768 devices in a mesh: dp: 96 (over z, x, core), tensor: 8 (over y).
Axes of the slice: x: 4, y: 8, z: 12, core: 2. Of those that a mesh axis runs over, the one named last changes fastest.
Arguments:
- patches: bfloat16 [98304, 1280], P('dp'), may hold values from -30 to 30
- qkv_weight: bfloat16 [1280, 3840], P(None, 'tensor'), may hold values from -1 to 1
- patch_counts: int32 [1536], replicated, may hold values from 1 to 64
- lend_dest: int32 [96], replicated, may hold values from 0 to 95, as said below
- lend_slot: int32 [96], replicated, may hold values from 0 to 15
- attn_grad: bfloat16 [98304, 1280], P('dp', 'tensor'), may hold values from -6 to 6
Outputs:
- context: bfloat16 [98304, 1280], P('dp', 'tensor')
- input_grad: bfloat16 [98304, 1280], P('dp', 'tensor')
- weight_grad: float32 [3840, 1280], P(('tensor', 'dp'))
The draws below stay inside these ranges and needn't reach their ends.
Inputs may be any that keep to these rules, and one draw needn't show every extreme that they name: `lend_dest`: a permutation of the data devices that maps every aligned group of 4 consecutive devices onto itself.
All inputs are finite; a program needn't handle non-finite values.
Results may differ from the reference program's by a relative error of at most 0.017.
Values may be sent and summed in bfloat16 or wider, within the bound.
No kernel may reach another device: no remote copies, remote signals or barrier semaphores. Data moves between devices by JAX's collectives and lax.ppermute only.
A program may use at most 64 MiB of HBM per device.

```python
import jax
import jax.numpy as jnp
from jax import lax

D = 1280
HEADS = 16
IMG_DEV = 16
BLOCK = 64
GROUP = 4
HD = 80
TOK_DEV = 1024
TOKENS = 98304
N_DP = 96
N_TENSOR = 8


def draw_patches(key, part):
    key = jax.random.fold_in(key, 11)
    normal_vals = jnp.clip(jax.random.normal(key, (TOKENS, D), jnp.float32), -6.0, 6.0)
    return normal_vals.astype(jnp.bfloat16)


def draw_qkv_weight(key, part):
    key = jax.random.fold_in(key, 12)
    key_query = jax.random.fold_in(key, 1)
    key_keys = jax.random.fold_in(key, 2)
    key_values = jax.random.fold_in(key, 3)
    factor = D ** (-0.5)
    query_part = jnp.clip(jax.random.normal(key_query, (D, HEADS, 1, HD), jnp.float32), -4.0, 4.0) * factor
    value_part = jnp.clip(jax.random.normal(key_values, (D, HEADS, 1, HD), jnp.float32), -4.0, 4.0) * factor
    keys_part = jnp.clip(jax.random.normal(key_keys, (D, HEADS, 1, HD), jnp.float32), -4.0, 4.0) * factor
    stacked = jnp.concatenate([query_part, keys_part, value_part], axis=2)
    return stacked.reshape(D, 3 * D).astype(jnp.bfloat16)


def draw_lend_dest(key, part):
    key = jax.random.fold_in(key, 13)
    group_count = N_DP // GROUP
    group_keys = jax.random.split(key, group_count)
    orders = jax.vmap(lambda one_key: jax.random.permutation(one_key, GROUP))(group_keys)
    offsets = jnp.arange(group_count, dtype=jnp.int32)[:, None] * GROUP
    return (orders.astype(jnp.int32) + offsets).reshape(N_DP).astype(jnp.int32)


def place_ends(values, stream_key, smallest, high):
    index_at = [jax.random.randint(jax.random.fold_in(stream_key, axis), (), 0, length) for axis, length in enumerate(values.shape)]
    longest = values.shape.index(max(values.shape))
    next_to = index_at[:longest] + [(index_at[longest] + 1) % values.shape[longest]] + index_at[longest + 1:]
    return values.at[tuple(index_at)].set(smallest).at[tuple(next_to)].set(high)


def levels(key, extent, cuts, low, top_value):
    factor_of, own = 1.0, jax.random.fold_in(key, 6)
    for position, parts in cuts:
        steps = jnp.exp(jax.random.uniform(jax.random.fold_in(own, position), (parts,), jnp.float32, low / len(cuts), top_value / len(cuts)))
        factor_of = factor_of * jnp.repeat(steps, extent[position] // parts).reshape([-1 if axis == position else 1 for axis in range(len(extent))])
    return factor_of


def centred(stream_key, dims, width, limit, cuts=(), kind=jnp.bfloat16):
    result = width * jax.random.normal(stream_key, dims, jnp.float32)
    if cuts:
        result = result * levels(stream_key, dims, cuts, -0.22, 0.18)
    return jnp.clip(result, -limit, limit).astype(kind)


def setup_inputs(seed: int = 0) -> dict:
    keys = jax.random.split(jax.random.key(seed), 7)
    return {
        "patches": draw_patches(jax.random.fold_in(keys[6], 71), 0),
        "qkv_weight": draw_qkv_weight(jax.random.fold_in(keys[6], 71), 0),
        "patch_counts": place_ends(jax.random.randint(keys[2], (N_DP * IMG_DEV,), 1, BLOCK + 1), jax.random.fold_in(keys[2], 1), 1, BLOCK).astype(jnp.int32),
        "lend_dest": draw_lend_dest(jax.random.fold_in(keys[6], 71), 0),
        "lend_slot": place_ends(jax.random.randint(keys[4], (N_DP,), 0, IMG_DEV), jax.random.fold_in(keys[4], 1), 0, IMG_DEV - 1).astype(jnp.int32),
        "attn_grad": centred(keys[5], (TOKENS, D), 1.0, 6.0, ((0, 96), (1, 8))),
    }


def block_attention(dest_rows, weight, live_counts, cotangent, head_count):
    row_count = dest_rows.shape[0]
    image_count = live_counts.shape[0]
    block_rows = row_count // image_count
    scaling = HD ** -0.5
    qkv_half = jnp.dot(dest_rows, weight, preferred_element_type=jnp.float32).astype(jnp.bfloat16)
    qkv_full = lax.optimization_barrier(qkv_half).astype(jnp.float32)
    qkv_full = qkv_full.reshape(image_count, block_rows, head_count, 3, HD)
    queries = qkv_full[:, :, :, 0]
    keys_all = qkv_full[:, :, :, 1]
    values_all = qkv_full[:, :, :, 2]
    positions = jnp.arange(block_rows, dtype=jnp.int32)
    keep_rows = positions[None, :] < live_counts[:, None]
    scores = jnp.einsum('ibhd,ijhd->ihbj', queries, keys_all) * scaling
    scores = jnp.where(keep_rows[:, None, None, :], scores, jnp.float32(-1e30))
    row_max = jnp.max(scores, axis=-1, keepdims=True)
    attn_prob = jnp.exp(scores - row_max)
    attn_prob = attn_prob / jnp.sum(attn_prob, axis=-1, keepdims=True)
    prob_half = lax.optimization_barrier(attn_prob.astype(jnp.bfloat16)).astype(jnp.float32)
    context = jnp.einsum('ihbj,ijhd->ibhd', prob_half, values_all)
    context = jnp.where(keep_rows[:, :, None, None], context, jnp.float32(0.0)).astype(jnp.bfloat16)
    grad_ctx = cotangent.reshape(image_count, block_rows, head_count, HD).astype(jnp.float32)
    grad_ctx = jnp.where(keep_rows[:, :, None, None], grad_ctx, jnp.float32(0.0))
    grad_value = jnp.einsum('ihbj,ibhd->ijhd', prob_half, grad_ctx).astype(jnp.bfloat16)
    grad_prob = jnp.einsum('ibhd,ijhd->ihbj', grad_ctx, values_all)
    grad_score = attn_prob * (grad_prob - jnp.sum(grad_prob * attn_prob, axis=-1, keepdims=True))
    score_half = lax.optimization_barrier(grad_score.astype(jnp.bfloat16)).astype(jnp.float32)
    grad_query = (jnp.einsum('ihbj,ijhd->ibhd', score_half, keys_all) * scaling).astype(jnp.bfloat16)
    grad_key = (jnp.einsum('ihbj,ibhd->ijhd', score_half, queries) * scaling).astype(jnp.bfloat16)
    grad_qkv = jnp.stack([grad_query, grad_key, grad_value], axis=3).reshape(row_count, head_count * 3 * HD)
    grouped_grad = grad_qkv.astype(jnp.float32).reshape(row_count, N_TENSOR, -1)
    grouped_weight = weight.astype(jnp.float32).reshape(weight.shape[0], N_TENSOR, -1)
    group_terms = jnp.einsum('rgc,dgc->grd', grouped_grad, grouped_weight)
    group_terms = lax.optimization_barrier(group_terms.astype(jnp.bfloat16)).astype(jnp.float32)
    grad_input = jnp.sum(group_terms, axis=0)
    grad_weight = lax.dot_general(grad_qkv, dest_rows, (((0,), (0,)), ((), ())), preferred_element_type=jnp.float32)
    return context.reshape(row_count, head_count * HD), grad_input.astype(jnp.bfloat16), grad_weight


def reference(patches, qkv_weight, patch_counts, lend_dest, lend_slot, attn_grad):
    devices = jnp.arange(N_DP, dtype=jnp.int32)
    images = patches.reshape(N_DP, IMG_DEV, BLOCK, D)
    count_table = patch_counts.reshape(N_DP, IMG_DEV)
    inverse = jnp.zeros((N_DP,), jnp.int32).at[lend_dest].set(devices)
    source_slot = lend_slot[inverse]
    dest_images = images.at[devices, lend_slot].set(images[inverse, source_slot])
    dest_counts = count_table.at[devices, lend_slot].set(count_table[inverse, source_slot])

    def device_step(weight_total, inputs):
        dest_rows, live_counts, cotangent = inputs
        context, grad_input, grad_weight = block_attention(dest_rows, qkv_weight, live_counts, cotangent, HEADS)
        return weight_total + grad_weight / TOK_DEV, (context, grad_input)

    weight_total, (contexts, grads) = lax.scan(
        device_step, jnp.zeros((3 * D, D), jnp.float32),
        (dest_images.reshape(N_DP, TOK_DEV, D), dest_counts, attn_grad.reshape(N_DP, TOK_DEV, D)))
    grads = grads.reshape(N_DP, IMG_DEV, BLOCK, D)
    back_blocks = grads[lend_dest, lend_slot[lend_dest]]
    home_grads = grads.at[devices, lend_slot].set(back_blocks)
    return contexts.reshape(TOKENS, D), home_grads.reshape(TOKENS, D), weight_total
```

```python
import functools

import jax
import jax.numpy as jnp
import numpy as np
from jax import lax
from jax.experimental import pallas as pl
from jax.experimental.pallas import tpu as pltpu
from jax.sharding import PartitionSpec as P

HEADS = 16
IMG_DEV = 16
BLOCK = 64
GROUP = 4
HD = 80
D = 1280
ROWS = 1024
SLOT = 128
COLS = 480
PADDED = 6 * SLOT
N_X = 4
N_CORE = 2
Z_NEAR = 4
Z_FAR = 3
BF16 = jnp.bfloat16
F32 = jnp.float32

NT = (((1,), (1,)), ((), ()))
NN = (((1,), (0,)), ((), ()))


def column_spread():
    spread = np.zeros((COLS, PADDED), np.float32)
    for slot in range(6):
        for d in range(HD):
            spread[slot * HD + d, slot * SLOT + d] = 1
    return spread.astype(jnp.bfloat16)


def head_spread():
    spread = np.zeros((2 * HD, 2 * SLOT), np.float32)
    for head in range(2):
        for d in range(HD):
            spread[head * HD + d, head * SLOT + d] = 1
    return spread.astype(jnp.bfloat16)


def owner_order():
    order = np.zeros((512, PADDED), np.float32)
    for c in range(COLS):
        z, x, core, i = c // 40, c % 40 // 10, c % 10 // 5, c % 5
        near, far = z % Z_NEAR, z // Z_NEAR
        order[core * 256 + x * 64 + near * 16 + far * 5 + i, c // HD * SLOT + c % HD] = 1
    return order.astype(jnp.bfloat16)


def dot(a, b, dims):
    return lax.dot_general(a, b, dims, preferred_element_type=F32)


def project_kernel(x_ref, w_ref, spread_ref, qkv_ref, wide_ref):
    @pl.when(pl.program_id(0) == 0)
    def _():
        wide_ref[...] = dot(w_ref[...], spread_ref[...], NN).astype(BF16)

    qkv_ref[...] = dot(x_ref[...], wide_ref[...], NN).astype(BF16)


def project(patches, weight, spread):
    step = 256
    return pl.pallas_call(
        project_kernel,
        grid=(ROWS // step,),
        in_specs=[
            pl.BlockSpec((step, D), lambda i: (i, 0)),
            pl.BlockSpec((D, COLS), lambda i: (0, 0)),
            pl.BlockSpec((COLS, PADDED), lambda i: (0, 0)),
        ],
        out_specs=[
            pl.BlockSpec((step, PADDED), lambda i: (i, 0)),
            pl.BlockSpec((D, PADDED), lambda i: (0, 0)),
        ],
        out_shape=[
            jax.ShapeDtypeStruct((ROWS, PADDED), BF16),
            jax.ShapeDtypeStruct((D, PADDED), BF16),
        ],
        cost_estimate=pl.CostEstimate(flops=2 * ROWS * D * PADDED, bytes_accessed=8_000_000, transcendentals=0),
        name="project",
    )(patches, weight, spread)


def attention_kernel(info_ref, counts_ref, qkv_ref, grad_ref, g0_ref, g1_ref, g2_ref, g3_ref, spread_ref, ctx_ref, dqkv_ref, lent_ref, held_ref):
    step = pl.program_id(0)
    pair = 2 * BLOCK
    scaling = HD ** (-0.5)
    my_slot = info_ref[0]
    pick = info_ref[1]
    here = my_slot // 2 == step
    inside = pl.multiple_of((my_slot % 2) * BLOCK, BLOCK)
    held_ref[...] = grad_ref[...]
    for index, block_ref in enumerate((g0_ref, g1_ref, g2_ref, g3_ref)):
        @pl.when(here & (pick == index))
        def _(block_ref=block_ref):
            held_ref[pl.ds(inside, BLOCK), :] = block_ref[...]

    first = counts_ref[2 * step]
    second = counts_ref[2 * step + 1]
    key = lax.broadcasted_iota(jnp.int32, (pair, pair), 0)
    query = lax.broadcasted_iota(jnp.int32, (pair, pair), 1)
    live = (key < jnp.minimum(first, BLOCK)) | ((key >= BLOCK) & (key < second + BLOCK))
    keep = live & ((key < BLOCK) == (query < BLOCK))
    live_rows = jnp.where(live, 1.0, 0.0)
    wide_grad = dot(held_ref[...], spread_ref[...], NN)
    wide_grad = (wide_grad * jnp.concatenate([live_rows] * 2, axis=1)).astype(BF16)
    contexts = []
    for head in range(2):
        base = head * 3 * SLOT
        q = qkv_ref[:, base : base + SLOT]
        k = qkv_ref[:, base + SLOT : base + 2 * SLOT]
        v = qkv_ref[:, base + 2 * SLOT : base + 3 * SLOT]
        g = wide_grad[:, head * SLOT : (head + 1) * SLOT]
        scores = jnp.where(keep, dot(k, q, NT) * scaling, -1e30)
        top = jnp.max(scores, axis=0, keepdims=True)
        e = jnp.exp(scores - top)
        p = e / jnp.sum(e, axis=0, keepdims=True)
        p_half = p.astype(BF16)
        contexts.append((dot(p.T.astype(BF16), v, NN) * live_rows).astype(BF16))
        dv = dot(p_half, g, NN)
        dp = dot(v, g, NT)
        ds = p * (dp - jnp.sum(dp * p, axis=0, keepdims=True))
        dq = dot(ds.T.astype(BF16), k, NN) * scaling
        dk = dot(ds.astype(BF16), q, NN) * scaling
        dqkv_ref[:, base : base + SLOT] = dq.astype(BF16)
        dqkv_ref[:, base + SLOT : base + 2 * SLOT] = dk.astype(BF16)
        dqkv_ref[:, base + 2 * SLOT : base + 3 * SLOT] = dv.astype(BF16)
    ctx_ref[...] = dot(jnp.concatenate(contexts, axis=1), spread_ref[...], NT).astype(BF16)

    @pl.when(here)
    def _():
        lent_ref[...] = ctx_ref[pl.ds(inside, BLOCK), :]


def attention(info, counts, qkv, grad, blocks, spread):
    pair = 2 * BLOCK
    width = 2 * HD
    whole = lambda i: (0, 0)
    smem = pl.BlockSpec(memory_space=pltpu.SMEM)
    return pl.pallas_call(
        attention_kernel,
        grid=(ROWS // pair,),
        in_specs=[
            smem,
            smem,
            pl.BlockSpec((pair, PADDED), lambda i: (i, 0)),
            pl.BlockSpec((pair, width), lambda i: (i, 0)),
        ]
        + [pl.BlockSpec((BLOCK, width), whole)] * 4
        + [pl.BlockSpec((width, 2 * SLOT), whole)],
        out_specs=[
            pl.BlockSpec((pair, width), lambda i: (i, 0)),
            pl.BlockSpec((pair, PADDED), lambda i: (i, 0)),
            pl.BlockSpec((BLOCK, width), whole),
        ],
        out_shape=[
            jax.ShapeDtypeStruct((ROWS, width), BF16),
            jax.ShapeDtypeStruct((ROWS, PADDED), BF16),
            jax.ShapeDtypeStruct((BLOCK, width), BF16),
        ],
        scratch_shapes=[pltpu.VMEM((pair, width), BF16)],
        cost_estimate=pl.CostEstimate(flops=400_000_000, bytes_accessed=4_000_000, transcendentals=300_000),
        name="attention",
    )(info, counts, qkv, grad, *blocks, spread)


def term_kernel(wide_ref, dqkv_ref, out_ref):
    out_ref[...] = dot(wide_ref[...], dqkv_ref[...], NT).astype(BF16)


def term(wide, dqkv):
    step = 320
    return pl.pallas_call(
        term_kernel,
        grid=(D // step,),
        in_specs=[pl.BlockSpec((step, PADDED), lambda i: (i, 0)), pl.BlockSpec((ROWS, PADDED), lambda i: (0, 0))],
        out_specs=pl.BlockSpec((step, ROWS), lambda i: (i, 0)),
        out_shape=jax.ShapeDtypeStruct((D, ROWS), BF16),
        cost_estimate=pl.CostEstimate(flops=2 * ROWS * D * PADDED, bytes_accessed=6_000_000, transcendentals=0),
        name="term",
    )(wide, dqkv)


def half_kernel(info_ref, order_ref, dqkv_ref, x_ref, out_ref):
    sorted_grad = dot(order_ref[...], dqkv_ref[...], NT).astype(BF16)
    out_ref[...] = (dot(sorted_grad, x_ref[...], NN) * (1.0 / ROWS)).astype(BF16)


def own_kernel(info_ref, order_ref, dqkv_ref, x_ref, other_ref, own_ref, s1_ref, s2_ref, s3_ref, held_ref):
    sorted_grad = dot(order_ref[...], dqkv_ref[...], NT).astype(BF16)
    held_ref[...] = dot(sorted_grad, x_ref[...], NN) * (1.0 / ROWS) + other_ref[...].astype(F32)
    rank = info_ref[3]
    for index, ref in enumerate((own_ref, s1_ref, s2_ref, s3_ref)):
        start = pl.multiple_of(lax.rem(rank + index, N_X) * 64, 64)
        ref[...] = held_ref[pl.ds(start, 64), :].astype(ref.dtype)


def half_specs(flip):
    def order_map(i, info):
        core = info[2]
        return (1 - core if flip else core, 0)

    return [
        pl.BlockSpec((256, PADDED), order_map),
        pl.BlockSpec((ROWS, PADDED), lambda i, info: (0, 0)),
        pl.BlockSpec((ROWS, D), lambda i, info: (0, 0)),
    ]


HALF_COST = pl.CostEstimate(flops=2 * 256 * ROWS * (D + PADDED), bytes_accessed=6_000_000, transcendentals=0)


def other_half(info, order, dqkv, patches):
    return pl.pallas_call(
        half_kernel,
        grid_spec=pltpu.PrefetchScalarGridSpec(
            num_scalar_prefetch=1,
            grid=(1,),
            in_specs=half_specs(True),
            out_specs=pl.BlockSpec((256, D), lambda i, info: (0, 0)),
        ),
        out_shape=jax.ShapeDtypeStruct((256, D), BF16),
        cost_estimate=HALF_COST,
        name="other_half",
    )(info, order, dqkv, patches)


def own_half(info, order, dqkv, patches, received):
    whole = lambda i, info: (0, 0)
    return pl.pallas_call(
        own_kernel,
        grid_spec=pltpu.PrefetchScalarGridSpec(
            num_scalar_prefetch=1,
            grid=(1,),
            in_specs=half_specs(False) + [pl.BlockSpec((256, D), whole)],
            out_specs=[pl.BlockSpec((64, D), whole)] * 4,
            scratch_shapes=[pltpu.VMEM((256, D), F32)],
        ),
        out_shape=[jax.ShapeDtypeStruct((64, D), F32)] + [jax.ShapeDtypeStruct((64, D), BF16)] * 3,
        cost_estimate=HALF_COST,
        name="own_half",
    )(info, order, dqkv, patches, received)


VMEM = pl.BlockSpec(memory_space=pltpu.VMEM)
SMEM = pl.BlockSpec(memory_space=pltpu.SMEM)


def near_kernel(info_ref, own_ref, a_ref, b_ref, c_ref, mine_ref, s1_ref, s2_ref, s3_ref, held_ref):
    held_ref[...] = own_ref[...] + a_ref[...].astype(F32) + b_ref[...].astype(F32) + c_ref[...].astype(F32)
    rank = info_ref[4]
    for index, ref in enumerate((mine_ref, s1_ref, s2_ref, s3_ref)):
        start = pl.multiple_of(lax.rem(rank + index, Z_NEAR) * 16, 16)
        ref[...] = held_ref[pl.ds(start, 16), :].astype(ref.dtype)


def near_sums(info, own, received):
    return pl.pallas_call(
        near_kernel,
        in_specs=[SMEM] + [VMEM] * 4,
        out_specs=[VMEM] * 4,
        out_shape=[jax.ShapeDtypeStruct((16, D), F32)] + [jax.ShapeDtypeStruct((16, D), BF16)] * 3,
        scratch_shapes=[pltpu.VMEM((64, D), F32)],
        name="near_sums",
    )(info, own, *received)


def far_kernel(info_ref, own_ref, a_ref, b_ref, c_ref, mine_ref, s1_ref, s2_ref):
    total = own_ref[...] + a_ref[...].astype(F32) + b_ref[...].astype(F32) + c_ref[...].astype(F32)
    rank = info_ref[5]
    rows = [total[0:8], jnp.concatenate([total[5:10], total[0:3]], axis=0), jnp.concatenate([total[10:15], total[0:3]], axis=0)]
    for index, ref in enumerate((mine_ref, s1_ref, s2_ref)):
        far = lax.rem(rank + index, Z_FAR)
        ref[...] = jnp.where(far == 0, rows[0], jnp.where(far == 1, rows[1], rows[2])).astype(ref.dtype)


def far_sums(info, own, received):
    return pl.pallas_call(
        far_kernel,
        in_specs=[SMEM] + [VMEM] * 4,
        out_specs=[VMEM] * 3,
        out_shape=[jax.ShapeDtypeStruct((8, D), F32)] + [jax.ShapeDtypeStruct((8, D), BF16)] * 2,
        name="far_sums",
    )(info, own, *received)


def last_kernel(own_ref, a_ref, b_ref, out_ref):
    total = own_ref[...] + a_ref[...].astype(F32) + b_ref[...].astype(F32)
    out_ref[...] = total[0:5]


def last_sum(own, received):
    return pl.pallas_call(
        last_kernel,
        in_specs=[VMEM] * 3,
        out_specs=VMEM,
        out_shape=jax.ShapeDtypeStruct((5, D), F32),
        name="last_sum",
    )(own, *received)


def turn_kernel(in_ref, out_ref):
    out_ref[...] = in_ref[...].astype(F32).T.astype(BF16)


def turn(columns):
    return pl.pallas_call(
        turn_kernel,
        in_specs=[VMEM],
        out_specs=VMEM,
        out_shape=jax.ShapeDtypeStruct((ROWS, 2 * HD), BF16),
        name="turn",
    )(columns)


def moved(value, target):
    return lax.ppermute(value, "dp", [(p, target(p)) for p in range(96)])


def xor_step(step):
    return lambda p: p ^ step


def x_step(step):
    return lambda p: p // 8 * 8 + ((p % 8 // 2 + step) % N_X) * 2 + p % 2


def near_step(step):
    def target(p):
        z = p // 8
        return (z // Z_NEAR * Z_NEAR + (z % Z_NEAR + step) % Z_NEAR) * 8 + p % 8

    return target


def far_step(step):
    def target(p):
        z = p // 8
        return ((z // Z_NEAR + step) % Z_FAR * Z_NEAR + z % Z_NEAR) * 8 + p % 8

    return target


def shards(patches, qkv_weight, patch_counts, lend_dest, lend_slot, attn_grad):
    my_rank = lax.axis_index("dp").astype(jnp.int32)
    ranks = jnp.arange(96, dtype=jnp.int32)
    my_slot = lend_slot[my_rank]
    pick = lend_dest[my_rank] ^ my_rank
    source = jnp.sum(jnp.where(lend_dest == my_rank, ranks, 0))
    z = my_rank // 8
    info = jnp.stack([my_slot, pick, my_rank % 2, my_rank % 8 // 2, z % Z_NEAR, z // Z_NEAR, source ^ my_rank, my_rank])
    counts = lax.dynamic_slice_in_dim(patch_counts, my_rank * IMG_DEV, IMG_DEV, 0)
    block = lax.dynamic_slice_in_dim(attn_grad, my_slot * BLOCK, BLOCK, 0)
    blocks = [block] + [moved(block, xor_step(s)) for s in range(1, GROUP)]
    qkv, wide = project(patches, qkv_weight, jnp.asarray(column_spread()))
    context, dqkv, lent = attention(info, counts, qkv, attn_grad, blocks, jnp.asarray(head_spread()))
    terms = term(wide, dqkv)
    summed = lax.psum_scatter(terms, "tensor", scatter_dimension=0, tiled=True)
    order = jnp.asarray(owner_order())
    received = moved(other_half(info, order, dqkv, patches), xor_step(1))
    own, *sends = own_half(info, order, dqkv, patches, received)
    own, *sends = near_sums(info, own, [moved(v, x_step(s + 1)) for s, v in enumerate(sends)])
    own, *sends = far_sums(info, own, [moved(v, near_step(s + 1)) for s, v in enumerate(sends)])
    weight_grad = last_sum(own, [moved(v, far_step(s + 1)) for s, v in enumerate(sends)])
    returned = lent
    for s in range(1, GROUP):
        returned = jnp.where(info[6] == s, moved(lent, xor_step(s)), returned)
    context = lax.dynamic_update_slice_in_dim(context, returned, my_slot * BLOCK, 0)
    return (context, turn(summed), weight_grad)


def solution(mesh):
    return jax.shard_map(
        shards,
        mesh=mesh,
        in_specs=(P("dp", None), P(None, "tensor"), P(), P(), P(), P("dp", "tensor")),
        out_specs=(P("dp", "tensor"), P("dp", "tensor"), P(("tensor", "dp"), None)),
        check_vma=False,
    )
```

```python
import jax
import jax.numpy as jnp
import numpy as np
from jax import lax
from jax.experimental import pallas as pl
from jax.experimental.pallas import tpu as pltpu
from jax.sharding import PartitionSpec as P

N_DP = 96
IMG_DEV = 16
BLOCK = 64
GROUP = 4
HD = 80
D = 1280
ROWS = 1024
COLS = 480
WIDTH = 2 * HD
PAIR = 2 * BLOCK
STEP = 2 * PAIR
N_X = 4
N_Z = 12
PACK = 16
BF16 = jnp.bfloat16
F32 = jnp.float32

NT = (((1,), (1,)), ((), ()))
NN = (((1,), (0,)), ((), ()))
TN = (((0,), (0,)), ((), ()))

VMEM = pl.BlockSpec(memory_space=pltpu.VMEM)
SMEM = pl.BlockSpec(memory_space=pltpu.SMEM)


def owner_order():
    order = np.zeros((512, COLS), np.float32)
    for c in range(COLS):
        z, x, core, i = c // 40, c % 40 // 10, c % 10 // 5, c % 5
        order[core * 256 + x * 64 + z * 5 + i, c] = 1
    return order.astype(jnp.bfloat16)


def dot(a, b, dims):
    return lax.dot_general(a, b, dims, preferred_element_type=F32)


def pick_kernel(rank_ref, slot_ref, in_ref, out_ref):
    out_ref[...] = in_ref[...]


def pick(rank, slots, grad):
    return pl.pallas_call(
        pick_kernel,
        grid_spec=pltpu.PrefetchScalarGridSpec(
            num_scalar_prefetch=2,
            grid=(1,),
            in_specs=[pl.BlockSpec((WIDTH, PAIR), lambda i, rank, slots: (0, slots[rank[0]] // 2))],
            out_specs=pl.BlockSpec((WIDTH, PAIR), lambda i, rank, slots: (0, 0)),
        ),
        out_shape=jax.ShapeDtypeStruct((WIDTH, PAIR), BF16),
        name="pick",
    )(rank, slots, grad)


def shifted(tile, flip):
    wide = tile.astype(F32)
    return jnp.where(flip, pltpu.roll(wide, BLOCK, 1), wide)


def block_kernel(rank_ref, slot_ref, dest_ref, counts_ref, w_ref, x_ref, grad_ref, gathered_ref, ctx_ref, dqkv_ref, term_ref, turned_ref):
    step = pl.program_id(0)
    scaling = HD ** (-0.5)

    @pl.when(step == 0)
    def _():
        for start in range(0, D, 256):
            turned_ref[start : start + 256, :] = w_ref[:, start : start + 256].astype(F32).T.astype(BF16)

    me = rank_ref[0]
    slot = slot_ref[me]
    host = dest_ref[me]
    lane = lax.broadcasted_iota(jnp.int32, (WIDTH, PAIR), 1)
    tile = gathered_ref[pl.ds(pl.multiple_of(lax.rem(host, GROUP) * WIDTH, 16), WIDTH), :]
    lent = shifted(tile, lax.rem(slot_ref[host], 2) != lax.rem(slot, 2))
    lent_lanes = (lane >= BLOCK) == (lax.rem(slot, 2) == 1)

    qkv = dot(w_ref[...], x_ref[...], NT).astype(BF16)
    key = lax.broadcasted_iota(jnp.int32, (PAIR, PAIR), 0)
    query = lax.broadcasted_iota(jnp.int32, (PAIR, PAIR), 1)
    same = (key < BLOCK) == (query < BLOCK)
    for pair in range(STEP // PAIR):
        columns = slice(pair * PAIR, (pair + 1) * PAIR)
        number = step * (STEP // PAIR) + pair
        first = counts_ref[me * IMG_DEV + 2 * number]
        second = counts_ref[me * IMG_DEV + 2 * number + 1]
        keep = ((key < first) | ((key >= BLOCK) & (key < second + BLOCK))) & same
        live = (lane < first) | ((lane >= BLOCK) & (lane < second + BLOCK))
        here = slot // 2 == number
        grad = jnp.where(lent_lanes & here, lent, grad_ref[:, columns].astype(F32))
        grad = jnp.where(live, grad, 0.0).astype(BF16)
        live = live[:HD]
        for head in range(2):
            base = head * 3 * HD
            q = qkv[base : base + HD, columns]
            k = qkv[base + HD : base + 2 * HD, columns]
            v = qkv[base + 2 * HD : base + 3 * HD, columns]
            g = grad[head * HD : (head + 1) * HD]
            scores = jnp.where(keep, dot(k, q, TN) * scaling, -1e30)
            e = jnp.exp(scores - jnp.max(scores, axis=0, keepdims=True))
            p = e / jnp.sum(e, axis=0, keepdims=True)
            p_half = p.astype(BF16)
            ctx_ref[head * HD : (head + 1) * HD, columns] = jnp.where(live, dot(v, p_half, NN), 0.0).astype(BF16)
            dv = dot(g, p_half, NT)
            dp = dot(v, g, TN)
            ds = (p * (dp - jnp.sum(dp * p, axis=0, keepdims=True))).astype(BF16)
            dq = dot(k, ds, NN) * scaling
            dk = dot(q, ds, NT) * scaling
            dqkv_ref[base : base + HD, columns] = dq.astype(BF16)
            dqkv_ref[base + HD : base + 2 * HD, columns] = dk.astype(BF16)
            dqkv_ref[base + 2 * HD : base + 3 * HD, columns] = dv.astype(BF16)
    term_ref[...] = dot(turned_ref[...], dqkv_ref[...], NN).astype(BF16)


def block(rank, slots, dest, counts, weight, patches, grad, gathered):
    return pl.pallas_call(
        block_kernel,
        grid=(ROWS // STEP,),
        in_specs=[
            SMEM,
            SMEM,
            SMEM,
            SMEM,
            pl.BlockSpec((COLS, D), lambda i: (0, 0)),
            pl.BlockSpec((STEP, D), lambda i: (i, 0)),
            pl.BlockSpec((WIDTH, STEP), lambda i: (0, i)),
            pl.BlockSpec((GROUP * WIDTH, PAIR), lambda i: (0, 0)),
        ],
        out_specs=[
            pl.BlockSpec((WIDTH, STEP), lambda i: (0, i)),
            pl.BlockSpec((COLS, STEP), lambda i: (0, i)),
            pl.BlockSpec((D, STEP), lambda i: (0, i)),
        ],
        out_shape=[
            jax.ShapeDtypeStruct((WIDTH, ROWS), BF16),
            jax.ShapeDtypeStruct((COLS, ROWS), BF16),
            jax.ShapeDtypeStruct((D, ROWS), BF16),
        ],
        scratch_shapes=[pltpu.VMEM((D, COLS), BF16)],
        cost_estimate=pl.CostEstimate(flops=6_000_000_000, bytes_accessed=9_000_000, transcendentals=300_000),
        name="block",
    )(rank, slots, dest, counts, weight, patches, grad, gathered)


def other_kernel(rank_ref, slot_ref, order_ref, dqkv_ref, x_ref, ctx_ref, out_ref):
    sorted_grad = dot(order_ref[...], dqkv_ref[...], NN).astype(BF16)
    out_ref[0:256, :] = (dot(sorted_grad, x_ref[...], NN) * (1.0 / ROWS)).astype(BF16)
    slot = slot_ref[rank_ref[0]]
    lent = shifted(ctx_ref[...], lax.rem(slot, 2) == 1).astype(BF16)
    for part in range(WIDTH // PACK):
        out_ref[256 : 256 + PACK, part * PAIR : (part + 1) * PAIR] = lent[part * PACK : (part + 1) * PACK]


def own_kernel(rank_ref, slot_ref, order_ref, dqkv_ref, x_ref, ctx_ref, other_ref, out_ref):
    sorted_grad = dot(order_ref[...], dqkv_ref[...], NN).astype(BF16)
    total = dot(sorted_grad, x_ref[...], NN) * (1.0 / ROWS) + other_ref[0:256, :].astype(F32)
    for x in range(N_X):
        out_ref[x, 0:64, :] = total[64 * x : 64 * (x + 1)].astype(BF16)
    slot = slot_ref[rank_ref[0]]
    lent = shifted(ctx_ref[...], lax.rem(slot, 2) == 1)
    lane = lax.broadcasted_iota(jnp.int32, (PACK, PAIR), 1)
    for part in range(WIDTH // PACK):
        columns = slice(part * PAIR, (part + 1) * PAIR)
        partner = pltpu.roll(other_ref[256 : 256 + PACK, columns].astype(F32), BLOCK, 1)
        both = jnp.where(lane < BLOCK, lent[part * PACK : (part + 1) * PACK], partner).astype(BF16)
        for x in range(N_X):
            out_ref[x, 64 : 64 + PACK, columns] = both


HALF_COST = pl.CostEstimate(flops=2 * 256 * ROWS * (D + COLS), bytes_accessed=6_000_000, transcendentals=0)


def half(kernel, flip, rank, slots, operands, shape, name):
    whole = lambda i, rank, slots: (0, 0)
    in_specs = [
        pl.BlockSpec((256, COLS), lambda i, rank, slots: ((1 - rank[0] % 2) if flip else rank[0] % 2, 0)),
        pl.BlockSpec((COLS, ROWS), whole),
        pl.BlockSpec((ROWS, D), whole),
        pl.BlockSpec((WIDTH, PAIR), lambda i, rank, slots: (0, slots[rank[0]] // 2)),
    ]
    if len(operands) == 5:
        in_specs.append(pl.BlockSpec((256 + PACK, D), whole))
    return pl.pallas_call(
        kernel,
        grid_spec=pltpu.PrefetchScalarGridSpec(
            num_scalar_prefetch=2,
            grid=(1,),
            in_specs=in_specs,
            out_specs=pl.BlockSpec(shape, lambda i, rank, slots: (0,) * len(shape)),
        ),
        out_shape=jax.ShapeDtypeStruct(shape, BF16),
        cost_estimate=HALF_COST,
        name=name,
    )(rank, slots, *operands)


def spread_kernel(rank_ref, slot_ref, dest_ref, in_ref, ctx_ref, out_ref, ctx_out_ref, held_ref):
    total = in_ref[0, 0:64, :].astype(F32)
    for x in range(1, N_X):
        total = total + in_ref[x, 0:64, :].astype(F32)
    held_ref[...] = total
    for z in range(N_Z):
        out_ref[z] = held_ref[5 * z : 5 * z + 8, :].astype(BF16)
    me = rank_ref[0]
    base = me // GROUP * GROUP
    source = base
    for k in range(1, GROUP):
        source = jnp.where(dest_ref[base + k] == me, base + k, source)
    slot = slot_ref[me]
    flip = (lax.rem(source, 2) != lax.rem(me, 2)) != (lax.rem(slot, 2) == 1)
    lane = lax.broadcasted_iota(jnp.int32, (PACK, PAIR), 1)
    mine = (lane >= BLOCK) == (lax.rem(slot, 2) == 1)
    x_source = lax.rem(source, 2 * N_X) // 2
    for part in range(WIDTH // PACK):
        rows = slice(part * PACK, (part + 1) * PACK)
        block_in = shifted(in_ref[x_source, 64 : 64 + PACK, part * PAIR : (part + 1) * PAIR], flip)
        ctx_out_ref[rows, :] = jnp.where(mine, block_in, ctx_ref[rows, :].astype(F32)).astype(BF16)


def spread(rank, slots, dest, received, ctx):
    tile = lambda i, rank, slots, dest: (0, slots[rank[0]] // 2)
    return pl.pallas_call(
        spread_kernel,
        grid_spec=pltpu.PrefetchScalarGridSpec(
            num_scalar_prefetch=3,
            grid=(1,),
            in_specs=[
                pl.BlockSpec((N_X, 64 + PACK, D), lambda i, rank, slots, dest: (0, 0, 0)),
                pl.BlockSpec((WIDTH, PAIR), tile),
            ],
            out_specs=[
                pl.BlockSpec((N_Z, 8, D), lambda i, rank, slots, dest: (0, 0, 0)),
                pl.BlockSpec((WIDTH, PAIR), tile),
            ],
            scratch_shapes=[pltpu.VMEM((64, D), F32)],
        ),
        out_shape=[jax.ShapeDtypeStruct((N_Z, 8, D), BF16), jax.ShapeDtypeStruct((WIDTH, ROWS), BF16)],
        input_output_aliases={4: 1},
        name="spread",
    )(rank, slots, dest, received, ctx)


def last_kernel(in_ref, out_ref):
    total = in_ref[0].astype(F32)
    for z in range(1, N_Z):
        total = total + in_ref[z].astype(F32)
    out_ref[...] = total[0:5]


def last_sum(received):
    return pl.pallas_call(
        last_kernel,
        in_specs=[VMEM],
        out_specs=VMEM,
        out_shape=jax.ShapeDtypeStruct((5, D), F32),
        name="last_sum",
    )(received)


def shards(patches, qkv_weight, patch_counts, lend_dest, lend_slot, attn_grad):
    rank = lax.axis_index("dp").astype(jnp.int32).reshape(1)
    grad = attn_grad.T
    weight = qkv_weight.T
    groups = [[base + k for k in range(GROUP)] for base in range(0, N_DP, GROUP)]
    x_groups = [[z * 8 + x * 2 + core for x in range(N_X)] for z in range(N_Z) for core in range(2)]
    z_groups = [[z * 8 + place for z in range(N_Z)] for place in range(8)]
    gathered = lax.all_gather(pick(rank, lend_slot, grad), "dp", axis=0, tiled=True, axis_index_groups=groups)
    ctx, dqkv, terms = block(rank, lend_slot, lend_dest, patch_counts, weight, patches, grad, gathered)
    summed = lax.psum_scatter(terms, "tensor", scatter_dimension=0, tiled=True)
    order = jnp.asarray(owner_order())
    operands = (order, dqkv, patches, ctx)
    sent = half(other_kernel, True, rank, lend_slot, operands, (256 + PACK, D), "other_half")
    received = lax.ppermute(sent, "dp", [(p, p ^ 1) for p in range(N_DP)])
    parts = half(own_kernel, False, rank, lend_slot, operands + (received,), (N_X, 64 + PACK, D), "own_half")
    parts = lax.all_to_all(parts, "dp", 0, 0, axis_index_groups=x_groups)
    parts, ctx = spread(rank, lend_slot, lend_dest, parts, ctx)
    parts = lax.all_to_all(parts, "dp", 0, 0, axis_index_groups=z_groups)
    return (ctx.T, summed.T, last_sum(parts))


def solution(mesh):
    return jax.shard_map(
        shards,
        mesh=mesh,
        in_specs=(P("dp", None), P(None, "tensor"), P(), P(), P(), P("dp", "tensor")),
        out_specs=(P("dp", "tensor"), P("dp", "tensor"), P(("tensor", "dp"), None)),
        check_vma=False,
    )
```

```python
import jax
import jax.numpy as jnp
import numpy as np
from jax import lax
from jax.experimental import pallas as pl
from jax.experimental.pallas import tpu as pltpu
from jax.sharding import PartitionSpec as P

N_DP = 96
IMG_DEV = 16
BLOCK = 64
GROUP = 4
HD = 80
D = 1280
ROWS = 1024
COLS = 480
WIDTH = 2 * HD
PAIR = 2 * BLOCK
STEP = 4 * PAIR
N_X = 4
N_Z = 12
PACK = 16
WIDE = 7 * PAIR
BF16 = jnp.bfloat16
F32 = jnp.float32

NT = (((1,), (1,)), ((), ()))
NN = (((1,), (0,)), ((), ()))
TN = (((0,), (0,)), ((), ()))

VMEM = pl.BlockSpec(memory_space=pltpu.VMEM)
SMEM = pl.BlockSpec(memory_space=pltpu.SMEM)
SMALL = pltpu.CompilerParams(vmem_limit_bytes=16 * 2**20)


def owner_order():
    order = np.zeros((512, COLS), np.float32)
    for c in range(COLS):
        z, x, core, i = c // 40, c % 40 // 10, c % 10 // 5, c % 5
        order[core * 256 + x * 64 + z * 5 + i, c] = 1
    return order.astype(jnp.bfloat16)


def dot(a, b, dims):
    return lax.dot_general(a, b, dims, preferred_element_type=F32)


def pick_kernel(rank_ref, slot_ref, in_ref, out_ref):
    out_ref[...] = in_ref[...]


def pick(rank, slots, grad):
    return pl.pallas_call(
        pick_kernel,
        grid_spec=pltpu.PrefetchScalarGridSpec(
            num_scalar_prefetch=2,
            grid=(1,),
            in_specs=[pl.BlockSpec((WIDTH, PAIR), lambda i, rank, slots: (0, slots[rank[0]] // 2))],
            out_specs=pl.BlockSpec((WIDTH, PAIR), lambda i, rank, slots: (0, 0)),
        ),
        out_shape=jax.ShapeDtypeStruct((WIDTH, PAIR), BF16),
        name="pick",
    )(rank, slots, grad)


def shifted(tile, flip):
    wide = tile.astype(F32)
    return jnp.where(flip, pltpu.roll(wide, BLOCK, 1), wide)


def block_kernel(rank_ref, slot_ref, dest_ref, counts_ref, w_ref, x_ref, grad_ref, gathered_ref, order_ref, ctx_ref, term_ref, own_ref, send_ref, dqkv_ref, turned_ref, sum_ref):
    step = pl.program_id(0)
    scaling = HD ** (-0.5)

    @pl.when(step == 0)
    def _():
        for start in range(0, D, 256):
            turned_ref[start : start + 256, :] = w_ref[:, start : start + 256].astype(F32).T.astype(BF16)

    me = rank_ref[0]
    slot = slot_ref[me]
    host = dest_ref[me]
    lane = lax.broadcasted_iota(jnp.int32, (WIDTH, PAIR), 1)
    tile = gathered_ref[pl.ds(pl.multiple_of(lax.rem(host, GROUP) * WIDTH, 16), WIDTH), :]
    lent = shifted(tile, lax.rem(slot_ref[host], 2) != lax.rem(slot, 2))
    lent_lanes = (lane >= BLOCK) == (lax.rem(slot, 2) == 1)

    qkv = dot(w_ref[...], x_ref[...], NT).astype(BF16)
    key = lax.broadcasted_iota(jnp.int32, (PAIR, PAIR), 0)
    query = lax.broadcasted_iota(jnp.int32, (PAIR, PAIR), 1)
    same = (key < BLOCK) == (query < BLOCK)
    keeps, lives, grads = [], [], []
    for pair in range(STEP // PAIR):
        columns = slice(pair * PAIR, (pair + 1) * PAIR)
        number = step * (STEP // PAIR) + pair
        first = counts_ref[me * IMG_DEV + 2 * number]
        second = counts_ref[me * IMG_DEV + 2 * number + 1]
        keeps.append(((key < first) | ((key >= BLOCK) & (key < second + BLOCK))) & same)
        live = (lane < first) | ((lane >= BLOCK) & (lane < second + BLOCK))
        here = slot // 2 == number
        grad = jnp.where(lent_lanes & here, lent, grad_ref[:, columns].astype(F32))
        grads.append(jnp.where(live, grad, 0.0).astype(BF16))
        lives.append(live[:HD])
    chains = [(pair, head) for pair in range(STEP // PAIR) for head in range(2)]

    def part(pair, head, which):
        base = head * 3 * HD + which * HD
        return qkv[base : base + HD, pair * PAIR : (pair + 1) * PAIR]

    q = [part(*c, 0) for c in chains]
    k = [part(*c, 1) for c in chains]
    v = [part(*c, 2) for c in chains]
    g = [grads[pair][head * HD : (head + 1) * HD] for pair, head in chains]
    many = range(len(chains))
    scores = [dot(k[c], q[c], TN) for c in many]
    dp = [dot(v[c], g[c], TN) for c in many]
    scores = [jnp.where(keeps[chains[c][0]], scores[c] * scaling, -1e30) for c in many]
    e = [jnp.exp(s - jnp.max(s, axis=0, keepdims=True)) for s in scores]
    p = [x / jnp.sum(x, axis=0, keepdims=True) for x in e]
    p_half = [x.astype(BF16) for x in p]
    ds = [(p[c] * (dp[c] - jnp.sum(dp[c] * p[c], axis=0, keepdims=True))).astype(BF16) for c in many]
    ctx = [dot(v[c], p_half[c], NN) for c in many]
    dv = [dot(g[c], p_half[c], NT) for c in many]
    dq = [dot(k[c], ds[c], NN) * scaling for c in many]
    dk = [dot(q[c], ds[c], NT) * scaling for c in many]
    for c, (pair, head) in enumerate(chains):
        columns = slice(pair * PAIR, (pair + 1) * PAIR)
        base = head * 3 * HD
        ctx_ref[head * HD : (head + 1) * HD, columns] = jnp.where(lives[pair], ctx[c], 0.0).astype(BF16)
        dqkv_ref[base : base + HD, columns] = dq[c].astype(BF16)
        dqkv_ref[base + HD : base + 2 * HD, columns] = dk[c].astype(BF16)
        dqkv_ref[base + 2 * HD : base + 3 * HD, columns] = dv[c].astype(BF16)
    term_ref[...] = dot(turned_ref[...], dqkv_ref[...], NN).astype(BF16)
    sorted_grad = dot(order_ref[...], dqkv_ref[...], NN).astype(BF16)
    part_sum = dot(sorted_grad, x_ref[...], NN)

    @pl.when(slot // (2 * STEP // PAIR) == step)
    def _():
        start = pl.multiple_of(lax.rem(slot // 2, STEP // PAIR) * PAIR, PAIR)
        mine = shifted(ctx_ref[:, pl.ds(start, PAIR)], lax.rem(slot, 2) == 1).astype(BF16)
        for piece in range(WIDTH // PACK):
            send_ref[256 : 256 + PACK, piece * PAIR : (piece + 1) * PAIR] = mine[piece * PACK : (piece + 1) * PACK]

    @pl.when(step == 0)
    def _():
        sum_ref[...] = part_sum

    @pl.when(step == 1)
    def _():
        sum_ref[...] = (sum_ref[...] + part_sum) * (1.0 / ROWS)
        core = lax.rem(me, 2)
        own_ref[...] = sum_ref[pl.ds(pl.multiple_of(core * 256, 256), 256), :].astype(BF16)
        send_ref[0:256, :] = sum_ref[pl.ds(pl.multiple_of((1 - core) * 256, 256), 256), :].astype(BF16)


def block(rank, slots, dest, counts, weight, patches, grad, gathered, order):
    whole = lambda i: (0, 0)
    return pl.pallas_call(
        block_kernel,
        grid=(ROWS // STEP,),
        in_specs=[
            SMEM,
            SMEM,
            SMEM,
            SMEM,
            pl.BlockSpec((COLS, D), whole),
            pl.BlockSpec((STEP, D), lambda i: (i, 0)),
            pl.BlockSpec((WIDTH, STEP), lambda i: (0, i)),
            pl.BlockSpec((GROUP * WIDTH, PAIR), whole),
            pl.BlockSpec((512, COLS), whole),
        ],
        out_specs=[
            pl.BlockSpec((WIDTH, STEP), lambda i: (0, i)),
            pl.BlockSpec((D, STEP), lambda i: (0, i)),
            pl.BlockSpec((256, D), whole),
            pl.BlockSpec((256 + PACK, D), whole),
        ],
        out_shape=[
            jax.ShapeDtypeStruct((WIDTH, ROWS), BF16),
            jax.ShapeDtypeStruct((D, ROWS), BF16),
            jax.ShapeDtypeStruct((256, D), BF16),
            jax.ShapeDtypeStruct((256 + PACK, D), BF16),
        ],
        scratch_shapes=[pltpu.VMEM((COLS, STEP), BF16), pltpu.VMEM((D, COLS), BF16), pltpu.VMEM((512, D), F32)],
        cost_estimate=pl.CostEstimate(flops=8_000_000_000, bytes_accessed=9_000_000, transcendentals=300_000),
        compiler_params=pltpu.CompilerParams(vmem_limit_bytes=57 * 2**20),
        name="block",
    )(rank, slots, dest, counts, weight, patches, grad, gathered, order)


def own_kernel(own_ref, sent_ref, other_ref, out_ref):
    for x in range(N_X):
        rows = slice(64 * x, 64 * (x + 1))
        out_ref[x, 0:64, :] = (own_ref[rows, :].astype(F32) + other_ref[rows, :].astype(F32)).astype(BF16)
    lane = lax.broadcasted_iota(jnp.int32, (PACK, PAIR), 1)
    for piece in range(WIDTH // PACK):
        columns = slice(piece * PAIR, (piece + 1) * PAIR)
        partner = pltpu.roll(other_ref[256 : 256 + PACK, columns].astype(F32), BLOCK, 1)
        both = jnp.where(lane < BLOCK, sent_ref[256 : 256 + PACK, columns].astype(F32), partner).astype(BF16)
        for x in range(N_X):
            out_ref[x, 64 : 64 + PACK, columns] = both


def own_half(own, sent, other):
    return pl.pallas_call(
        own_kernel,
        in_specs=[VMEM] * 3,
        out_specs=VMEM,
        out_shape=jax.ShapeDtypeStruct((N_X, 64 + PACK, D), BF16),
        compiler_params=SMALL,
        name="own_half",
    )(own, sent, other)


def spread_kernel(rank_ref, slot_ref, dest_ref, in_ref, ctx_ref, out_ref, ctx_out_ref, held_ref):
    total = in_ref[0, 0:64, :].astype(F32)
    for x in range(1, N_X):
        total = total + in_ref[x, 0:64, :].astype(F32)
    held_ref[...] = total
    upper = lax.broadcasted_iota(jnp.int32, (8, PAIR), 0) < 5
    for z in range(N_Z):
        rows = held_ref[5 * z : 5 * z + 8, :]
        late = rows[:, WIDE:]
        low, high = pltpu.roll(late, 5, 0), pltpu.roll(late, 2, 0)
        for piece in range(WIDE // PAIR):
            front = rows[:, piece * PAIR : (piece + 1) * PAIR]
            if piece < 6:
                source_piece = (high if piece % 2 else low)[:, piece // 2 * PAIR : (piece // 2 + 1) * PAIR]
                front = jnp.where(upper, front, source_piece)
            out_ref[z, :, piece * PAIR : (piece + 1) * PAIR] = front.astype(BF16)
    me = rank_ref[0]
    base = me // GROUP * GROUP
    source = base
    for k in range(1, GROUP):
        source = jnp.where(dest_ref[base + k] == me, base + k, source)
    slot = slot_ref[me]
    flip = (lax.rem(source, 2) != lax.rem(me, 2)) != (lax.rem(slot, 2) == 1)
    lane = lax.broadcasted_iota(jnp.int32, (PACK, PAIR), 1)
    mine = (lane >= BLOCK) == (lax.rem(slot, 2) == 1)
    x_source = lax.rem(source, 2 * N_X) // 2
    for part in range(WIDTH // PACK):
        rows = slice(part * PACK, (part + 1) * PACK)
        block_in = shifted(in_ref[x_source, 64 : 64 + PACK, part * PAIR : (part + 1) * PAIR], flip)
        ctx_out_ref[rows, :] = jnp.where(mine, block_in, ctx_ref[rows, :].astype(F32)).astype(BF16)


def spread(rank, slots, dest, received, ctx):
    tile = lambda i, rank, slots, dest: (0, slots[rank[0]] // 2)
    return pl.pallas_call(
        spread_kernel,
        grid_spec=pltpu.PrefetchScalarGridSpec(
            num_scalar_prefetch=3,
            grid=(1,),
            in_specs=[
                pl.BlockSpec((N_X, 64 + PACK, D), lambda i, rank, slots, dest: (0, 0, 0)),
                pl.BlockSpec((WIDTH, PAIR), tile),
            ],
            out_specs=[
                pl.BlockSpec((N_Z, 8, WIDE), lambda i, rank, slots, dest: (0, 0, 0)),
                pl.BlockSpec((WIDTH, PAIR), tile),
            ],
            scratch_shapes=[pltpu.VMEM((64, D), F32)],
        ),
        out_shape=[jax.ShapeDtypeStruct((N_Z, 8, WIDE), BF16), jax.ShapeDtypeStruct((WIDTH, ROWS), BF16)],
        input_output_aliases={4: 1},
        compiler_params=SMALL,
        name="spread",
    )(rank, slots, dest, received, ctx)


def last_kernel(in_ref, out_ref):
    total = in_ref[0].astype(F32)
    for z in range(1, N_Z):
        total = total + in_ref[z].astype(F32)
    out_ref[:, 0:WIDE] = total[0:5]
    upper = lax.broadcasted_iota(jnp.int32, (8, PAIR), 0) < 3
    for piece in range(3):
        low = pltpu.roll(total[:, 2 * piece * PAIR : (2 * piece + 1) * PAIR], 3, 0)
        high = pltpu.roll(total[:, (2 * piece + 1) * PAIR : (2 * piece + 2) * PAIR], 6, 0)
        out_ref[:, WIDE + piece * PAIR : WIDE + (piece + 1) * PAIR] = jnp.where(upper, low, high)[0:5]


def last_sum(received):
    return pl.pallas_call(
        last_kernel,
        in_specs=[VMEM],
        out_specs=VMEM,
        out_shape=jax.ShapeDtypeStruct((5, D), F32),
        compiler_params=SMALL,
        name="last_sum",
    )(received)


def shards(patches, qkv_weight, patch_counts, lend_dest, lend_slot, attn_grad):
    rank = lax.axis_index("dp").astype(jnp.int32).reshape(1)
    grad = attn_grad.T
    weight = qkv_weight.T
    groups = [[base + k for k in range(GROUP)] for base in range(0, N_DP, GROUP)]
    x_groups = [[z * 8 + x * 2 + core for x in range(N_X)] for z in range(N_Z) for core in range(2)]
    z_groups = [[z * 8 + place for z in range(N_Z)] for place in range(8)]
    gathered = lax.all_gather(pick(rank, lend_slot, grad), "dp", axis=0, tiled=True, axis_index_groups=groups)
    order = jnp.asarray(owner_order())
    ctx, terms, own, sent = block(rank, lend_slot, lend_dest, patch_counts, weight, patches, grad, gathered, order)
    summed = lax.psum_scatter(terms, "tensor", scatter_dimension=0, tiled=True)
    received = lax.ppermute(sent, "dp", [(p, p ^ 1) for p in range(N_DP)])
    parts = own_half(own, sent, received)
    parts = lax.all_to_all(parts, "dp", 0, 0, axis_index_groups=x_groups)
    parts, ctx = spread(rank, lend_slot, lend_dest, parts, ctx)
    parts = lax.all_to_all(parts, "dp", 0, 0, axis_index_groups=z_groups)
    return (ctx.T, summed.T, last_sum(parts))


def solution(mesh):
    return jax.shard_map(
        shards,
        mesh=mesh,
        in_specs=(P("dp", None), P(None, "tensor"), P(), P(), P(), P("dp", "tensor")),
        out_specs=(P("dp", "tensor"), P("dp", "tensor"), P(("tensor", "dp"), None)),
        check_vma=False,
    )
```

```python
import jax
import jax.numpy as jnp
import numpy as np
from jax import lax
from jax.experimental import pallas as pl
from jax.experimental.pallas import tpu as pltpu
from jax.sharding import PartitionSpec as P

N_DP = 96
IMG_DEV = 16
BLOCK = 64
GROUP = 4
HD = 80
D = 1280
ROWS = 1024
COLS = 480
WIDTH = 2 * HD
PAIR = 2 * BLOCK
STEP = 4 * PAIR
N_X = 4
N_Z = 12
PACK = 16
WIDE = 7 * PAIR
BF16 = jnp.bfloat16
F32 = jnp.float32

NT = (((1,), (1,)), ((), ()))
NN = (((1,), (0,)), ((), ()))
TN = (((0,), (0,)), ((), ()))

VMEM = pl.BlockSpec(memory_space=pltpu.VMEM)
SMEM = pl.BlockSpec(memory_space=pltpu.SMEM)
SMALL = pltpu.CompilerParams(vmem_limit_bytes=16 * 2**20)


def owner_order():
    order = np.zeros((512, COLS), np.float32)
    for c in range(COLS):
        z, x, core, i = c // 40, c % 40 // 10, c % 10 // 5, c % 5
        order[core * 256 + x * 64 + z * 5 + i, c] = 1
    return order.astype(jnp.bfloat16)


def dot(a, b, dims):
    return lax.dot_general(a, b, dims, preferred_element_type=F32)


def pick_kernel(rank_ref, slot_ref, in_ref, out_ref):
    out_ref[...] = in_ref[...]


def pick(rank, slots, grad):
    return pl.pallas_call(
        pick_kernel,
        grid_spec=pltpu.PrefetchScalarGridSpec(
            num_scalar_prefetch=2,
            grid=(1,),
            in_specs=[pl.BlockSpec((WIDTH, PAIR), lambda i, rank, slots: (0, slots[rank[0]] // 2))],
            out_specs=pl.BlockSpec((WIDTH, PAIR), lambda i, rank, slots: (0, 0)),
        ),
        out_shape=jax.ShapeDtypeStruct((WIDTH, PAIR), BF16),
        name="pick",
    )(rank, slots, grad)


def shifted(tile, flip):
    wide = tile.astype(F32)
    return jnp.where(flip, pltpu.roll(wide, BLOCK, 1), wide)


def block_kernel(rank_ref, slot_ref, dest_ref, counts_ref, w_ref, x_ref, grad_ref, gathered_ref, ctx_ref, term_ref, dqkv_ref, pack_ref, turned_ref):
    step = pl.program_id(0)
    scaling = HD ** (-0.5)

    @pl.when(step == 0)
    def _():
        for start in range(0, D, 256):
            turned_ref[start : start + 256, :] = w_ref[:, start : start + 256].astype(F32).T.astype(BF16)

    me = rank_ref[0]
    slot = slot_ref[me]
    host = dest_ref[me]
    lane = lax.broadcasted_iota(jnp.int32, (WIDTH, PAIR), 1)
    tile = gathered_ref[pl.ds(pl.multiple_of(lax.rem(host, GROUP) * WIDTH, 16), WIDTH), :]
    lent = shifted(tile, lax.rem(slot_ref[host], 2) != lax.rem(slot, 2))
    lent_lanes = (lane >= BLOCK) == (lax.rem(slot, 2) == 1)

    qkv = dot(w_ref[...], x_ref[...], NT).astype(BF16)
    key = lax.broadcasted_iota(jnp.int32, (PAIR, PAIR), 0)
    query = lax.broadcasted_iota(jnp.int32, (PAIR, PAIR), 1)
    same = (key < BLOCK) == (query < BLOCK)
    keeps, lives, grads = [], [], []
    for pair in range(STEP // PAIR):
        columns = slice(pair * PAIR, (pair + 1) * PAIR)
        number = step * (STEP // PAIR) + pair
        first = counts_ref[me * IMG_DEV + 2 * number]
        second = counts_ref[me * IMG_DEV + 2 * number + 1]
        keeps.append(((key < first) | ((key >= BLOCK) & (key < second + BLOCK))) & same)
        live = (lane < first) | ((lane >= BLOCK) & (lane < second + BLOCK))
        here = slot // 2 == number
        grad = jnp.where(lent_lanes & here, lent, grad_ref[:, columns].astype(F32))
        grads.append(jnp.where(live, grad, 0.0).astype(BF16))
        lives.append(live[:HD])
    chains = [(pair, head) for pair in range(STEP // PAIR) for head in range(2)]

    def part(pair, head, which):
        base = head * 3 * HD + which * HD
        return qkv[base : base + HD, pair * PAIR : (pair + 1) * PAIR]

    q = [part(*c, 0) for c in chains]
    k = [part(*c, 1) for c in chains]
    v = [part(*c, 2) for c in chains]
    g = [grads[pair][head * HD : (head + 1) * HD] for pair, head in chains]
    many = range(len(chains))
    scores = [dot(k[c], q[c], TN) for c in many]
    dp = [dot(v[c], g[c], TN) for c in many]
    scores = [jnp.where(keeps[chains[c][0]], scores[c] * scaling, -1e30) for c in many]
    e = [jnp.exp(s - jnp.max(s, axis=0, keepdims=True)) for s in scores]
    p = [x / jnp.sum(x, axis=0, keepdims=True) for x in e]
    p_half = [x.astype(BF16) for x in p]
    ds = [(p[c] * (dp[c] - jnp.sum(dp[c] * p[c], axis=0, keepdims=True))).astype(BF16) for c in many]
    ctx = [dot(v[c], p_half[c], NN) for c in many]
    dv = [dot(g[c], p_half[c], NT) for c in many]
    dq = [dot(k[c], ds[c], NN) * scaling for c in many]
    dk = [dot(q[c], ds[c], NT) * scaling for c in many]
    for c, (pair, head) in enumerate(chains):
        columns = slice(pair * PAIR, (pair + 1) * PAIR)
        base = head * 3 * HD
        ctx_ref[head * HD : (head + 1) * HD, columns] = jnp.where(lives[pair], ctx[c], 0.0).astype(BF16)
        dqkv_ref[base : base + HD, columns] = dq[c].astype(BF16)
        dqkv_ref[base + HD : base + 2 * HD, columns] = dk[c].astype(BF16)
        dqkv_ref[base + 2 * HD : base + 3 * HD, columns] = dv[c].astype(BF16)
    term_ref[...] = dot(turned_ref[...], dqkv_ref[...], NN).astype(BF16)

    @pl.when(slot // (2 * STEP // PAIR) == step)
    def _():
        start = pl.multiple_of(lax.rem(slot // 2, STEP // PAIR) * PAIR, PAIR)
        mine = shifted(ctx_ref[:, pl.ds(start, PAIR)], lax.rem(slot, 2) == 1).astype(BF16)
        for piece in range(WIDTH // PACK):
            pack_ref[:, piece * PAIR : (piece + 1) * PAIR] = mine[piece * PACK : (piece + 1) * PACK]


def block(rank, slots, dest, counts, weight, patches, grad, gathered):
    whole = lambda i: (0, 0)
    return pl.pallas_call(
        block_kernel,
        grid=(ROWS // STEP,),
        in_specs=[
            SMEM,
            SMEM,
            SMEM,
            SMEM,
            pl.BlockSpec((COLS, D), whole),
            pl.BlockSpec((STEP, D), lambda i: (i, 0)),
            pl.BlockSpec((WIDTH, STEP), lambda i: (0, i)),
            pl.BlockSpec((GROUP * WIDTH, PAIR), whole),
        ],
        out_specs=[
            pl.BlockSpec((WIDTH, STEP), lambda i: (0, i)),
            pl.BlockSpec((D, STEP), lambda i: (0, i)),
            pl.BlockSpec((COLS, STEP), lambda i: (0, i)),
            pl.BlockSpec((PACK, D), whole),
        ],
        out_shape=[
            jax.ShapeDtypeStruct((WIDTH, ROWS), BF16),
            jax.ShapeDtypeStruct((D, ROWS), BF16),
            jax.ShapeDtypeStruct((COLS, ROWS), BF16),
            jax.ShapeDtypeStruct((PACK, D), BF16),
        ],
        scratch_shapes=[pltpu.VMEM((D, COLS), BF16)],
        cost_estimate=pl.CostEstimate(flops=6_000_000_000, bytes_accessed=9_000_000, transcendentals=300_000),
        compiler_params=pltpu.CompilerParams(vmem_limit_bytes=57 * 2**20),
        name="block",
    )(rank, slots, dest, counts, weight, patches, grad, gathered)


def sums_kernel(rank_ref, order_ref, dqkv_ref, x_ref, pack_ref, own_ref, send_ref):
    core = lax.rem(rank_ref[0], 2)
    for which, ref in ((1 - core, send_ref), (core, own_ref)):
        order = order_ref[pl.ds(pl.multiple_of(which * 256, 256), 256), :]
        sorted_grad = dot(order, dqkv_ref[...], NN).astype(BF16)
        ref[0:256, :] = (dot(sorted_grad, x_ref[...], NN) * (1.0 / ROWS)).astype(BF16)
    send_ref[256 : 256 + PACK, :] = pack_ref[...]


def sums(rank, order, dqkv, patches, pack):
    return pl.pallas_call(
        sums_kernel,
        in_specs=[SMEM] + [VMEM] * 4,
        out_specs=[VMEM] * 2,
        out_shape=[jax.ShapeDtypeStruct((256, D), BF16), jax.ShapeDtypeStruct((256 + PACK, D), BF16)],
        cost_estimate=pl.CostEstimate(flops=2_000_000_000, bytes_accessed=6_000_000, transcendentals=0),
        compiler_params=SMALL,
        name="sums",
    )(rank, order, dqkv, patches, pack)


def own_kernel(own_ref, pack_ref, other_ref, out_ref):
    for x in range(N_X):
        rows = slice(64 * x, 64 * (x + 1))
        out_ref[x, 0:64, :] = (own_ref[rows, :].astype(F32) + other_ref[rows, :].astype(F32)).astype(BF16)
    lane = lax.broadcasted_iota(jnp.int32, (PACK, PAIR), 1)
    for piece in range(WIDTH // PACK):
        columns = slice(piece * PAIR, (piece + 1) * PAIR)
        partner = pltpu.roll(other_ref[256 : 256 + PACK, columns].astype(F32), BLOCK, 1)
        both = jnp.where(lane < BLOCK, pack_ref[:, columns].astype(F32), partner).astype(BF16)
        for x in range(N_X):
            out_ref[x, 64 : 64 + PACK, columns] = both


def own_half(own, pack, other):
    return pl.pallas_call(
        own_kernel,
        in_specs=[VMEM] * 3,
        out_specs=VMEM,
        out_shape=jax.ShapeDtypeStruct((N_X, 64 + PACK, D), BF16),
        compiler_params=SMALL,
        name="own_half",
    )(own, pack, other)


def spread_kernel(rank_ref, slot_ref, dest_ref, in_ref, ctx_ref, out_ref, ctx_out_ref, held_ref):
    total = in_ref[0, 0:64, :].astype(F32)
    for x in range(1, N_X):
        total = total + in_ref[x, 0:64, :].astype(F32)
    held_ref[...] = total
    upper = lax.broadcasted_iota(jnp.int32, (8, PAIR), 0) < 5
    for z in range(N_Z):
        rows = held_ref[5 * z : 5 * z + 8, :]
        late = rows[:, WIDE:]
        low, high = pltpu.roll(late, 5, 0), pltpu.roll(late, 2, 0)
        for piece in range(WIDE // PAIR):
            front = rows[:, piece * PAIR : (piece + 1) * PAIR]
            if piece < 6:
                source_piece = (high if piece % 2 else low)[:, piece // 2 * PAIR : (piece // 2 + 1) * PAIR]
                front = jnp.where(upper, front, source_piece)
            out_ref[z, :, piece * PAIR : (piece + 1) * PAIR] = front.astype(BF16)
    me = rank_ref[0]
    base = me // GROUP * GROUP
    source = base
    for k in range(1, GROUP):
        source = jnp.where(dest_ref[base + k] == me, base + k, source)
    slot = slot_ref[me]
    flip = (lax.rem(source, 2) != lax.rem(me, 2)) != (lax.rem(slot, 2) == 1)
    lane = lax.broadcasted_iota(jnp.int32, (PACK, PAIR), 1)
    mine = (lane >= BLOCK) == (lax.rem(slot, 2) == 1)
    x_source = lax.rem(source, 2 * N_X) // 2
    for part in range(WIDTH // PACK):
        rows = slice(part * PACK, (part + 1) * PACK)
        block_in = shifted(in_ref[x_source, 64 : 64 + PACK, part * PAIR : (part + 1) * PAIR], flip)
        ctx_out_ref[rows, :] = jnp.where(mine, block_in, ctx_ref[rows, :].astype(F32)).astype(BF16)


def spread(rank, slots, dest, received, ctx):
    tile = lambda i, rank, slots, dest: (0, slots[rank[0]] // 2)
    return pl.pallas_call(
        spread_kernel,
        grid_spec=pltpu.PrefetchScalarGridSpec(
            num_scalar_prefetch=3,
            grid=(1,),
            in_specs=[
                pl.BlockSpec((N_X, 64 + PACK, D), lambda i, rank, slots, dest: (0, 0, 0)),
                pl.BlockSpec((WIDTH, PAIR), tile),
            ],
            out_specs=[
                pl.BlockSpec((N_Z, 8, WIDE), lambda i, rank, slots, dest: (0, 0, 0)),
                pl.BlockSpec((WIDTH, PAIR), tile),
            ],
            scratch_shapes=[pltpu.VMEM((64, D), F32)],
        ),
        out_shape=[jax.ShapeDtypeStruct((N_Z, 8, WIDE), BF16), jax.ShapeDtypeStruct((WIDTH, ROWS), BF16)],
        input_output_aliases={4: 1},
        compiler_params=SMALL,
        name="spread",
    )(rank, slots, dest, received, ctx)


def last_kernel(in_ref, out_ref):
    total = in_ref[0].astype(F32)
    for z in range(1, N_Z):
        total = total + in_ref[z].astype(F32)
    out_ref[:, 0:WIDE] = total[0:5]
    upper = lax.broadcasted_iota(jnp.int32, (8, PAIR), 0) < 3
    for piece in range(3):
        low = pltpu.roll(total[:, 2 * piece * PAIR : (2 * piece + 1) * PAIR], 3, 0)
        high = pltpu.roll(total[:, (2 * piece + 1) * PAIR : (2 * piece + 2) * PAIR], 6, 0)
        out_ref[:, WIDE + piece * PAIR : WIDE + (piece + 1) * PAIR] = jnp.where(upper, low, high)[0:5]


def last_sum(received):
    return pl.pallas_call(
        last_kernel,
        in_specs=[VMEM],
        out_specs=VMEM,
        out_shape=jax.ShapeDtypeStruct((5, D), F32),
        compiler_params=SMALL,
        name="last_sum",
    )(received)


def shards(patches, qkv_weight, patch_counts, lend_dest, lend_slot, attn_grad):
    rank = lax.axis_index("dp").astype(jnp.int32).reshape(1)
    grad = attn_grad.T
    weight = qkv_weight.T
    groups = [[base + k for k in range(GROUP)] for base in range(0, N_DP, GROUP)]
    x_groups = [[z * 8 + x * 2 + core for x in range(N_X)] for z in range(N_Z) for core in range(2)]
    z_groups = [[z * 8 + place for z in range(N_Z)] for place in range(8)]
    gathered = lax.all_gather(pick(rank, lend_slot, grad), "dp", axis=0, tiled=True, axis_index_groups=groups)
    ctx, terms, dqkv, pack = block(rank, lend_slot, lend_dest, patch_counts, weight, patches, grad, gathered)
    summed = lax.psum_scatter(terms, "tensor", scatter_dimension=0, tiled=True)
    own, sent = sums(rank, jnp.asarray(owner_order()), dqkv, patches, pack)
    received = lax.ppermute(sent, "dp", [(p, p ^ 1) for p in range(N_DP)])
    parts = own_half(own, pack, received)
    parts = lax.all_to_all(parts, "dp", 0, 0, axis_index_groups=x_groups)
    parts, ctx = spread(rank, lend_slot, lend_dest, parts, ctx)
    parts = lax.all_to_all(parts, "dp", 0, 0, axis_index_groups=z_groups)
    return (ctx.T, summed.T, last_sum(parts))


def solution(mesh):
    return jax.shard_map(
        shards,
        mesh=mesh,
        in_specs=(P("dp", None), P(None, "tensor"), P(), P(), P(), P("dp", "tensor")),
        out_specs=(P("dp", "tensor"), P("dp", "tensor"), P(("tensor", "dp"), None)),
        check_vma=False,
    )
```

```python
import jax
import jax.numpy as jnp
import numpy as np
from jax import lax
from jax.experimental import pallas as pl
from jax.experimental.pallas import tpu as pltpu
from jax.sharding import PartitionSpec as P

N_DP = 96
IMG_DEV = 16
BLOCK = 64
GROUP = 4
HD = 80
D = 1280
ROWS = 1024
COLS = 480
WIDTH = 2 * HD
PAIR = 2 * BLOCK
STEP = 4 * PAIR
CUT = 256
N_X = 4
N_Z = 12
PACK = 16
WIDE = 7 * PAIR
BF16 = jnp.bfloat16
F32 = jnp.float32

NT = (((1,), (1,)), ((), ()))
NN = (((1,), (0,)), ((), ()))
TN = (((0,), (0,)), ((), ()))

VMEM = pl.BlockSpec(memory_space=pltpu.VMEM)
SMEM = pl.BlockSpec(memory_space=pltpu.SMEM)
HBM = pl.BlockSpec(memory_space=pltpu.HBM)
SMALL = pltpu.CompilerParams(vmem_limit_bytes=16 * 2**20)


def owner_order():
    order = np.zeros((512, COLS), np.float32)
    for c in range(COLS):
        z, x, core, i = c // 40, c % 40 // 10, c % 10 // 5, c % 5
        order[core * 256 + x * 64 + z * 5 + i, c] = 1
    return order.astype(jnp.bfloat16)


def dot(a, b, dims):
    return lax.dot_general(a, b, dims, preferred_element_type=F32)


def pick_kernel(rank_ref, slot_ref, in_ref, out_ref):
    upper = lax.rem(slot_ref[rank_ref[0]], 2) == 1
    lane = lax.broadcasted_iota(jnp.int32, (HD, PAIR), 1)
    left = shifted(in_ref[0:HD, :], upper)
    right = shifted(in_ref[HD:WIDTH, :], jnp.logical_not(upper))
    out_ref[...] = jnp.where(lane < BLOCK, left, right).astype(BF16)


def pick(rank, slots, grad):
    return pl.pallas_call(
        pick_kernel,
        grid_spec=pltpu.PrefetchScalarGridSpec(
            num_scalar_prefetch=2,
            grid=(1,),
            in_specs=[pl.BlockSpec((WIDTH, PAIR), lambda i, rank, slots: (0, slots[rank[0]] // 2))],
            out_specs=pl.BlockSpec((HD, PAIR), lambda i, rank, slots: (0, 0)),
        ),
        out_shape=jax.ShapeDtypeStruct((HD, PAIR), BF16),
        cost_estimate=pl.CostEstimate(flops=20_000_000_000, bytes_accessed=40_000_000, transcendentals=0),
        compiler_params=pltpu.CompilerParams(vmem_limit_bytes=60400 * 1024),
        name="pick",
    )(rank, slots, grad)


def shifted(tile, flip):
    wide = tile.astype(F32)
    return jnp.where(flip, pltpu.roll(wide, BLOCK, 1), wide)


def attend(me, slot, group, lent, counts_ref, grad_buf, qkv_buf, ctx_buf, dqkv_buf):
    scaling = HD ** (-0.5)
    lane = lax.broadcasted_iota(jnp.int32, (WIDTH, PAIR), 1)
    lent_lanes = (lane >= BLOCK) == (lax.rem(slot, 2) == 1)
    key = lax.broadcasted_iota(jnp.int32, (PAIR, PAIR), 0)
    query = lax.broadcasted_iota(jnp.int32, (PAIR, PAIR), 1)
    same = (key < BLOCK) == (query < BLOCK)
    pairs = range(group * (STEP // PAIR), (group + 1) * (STEP // PAIR))
    keeps, lives, grads = {}, {}, {}
    for pair in pairs:
        columns = slice(pair * PAIR, (pair + 1) * PAIR)
        first = counts_ref[me * IMG_DEV + 2 * pair]
        second = counts_ref[me * IMG_DEV + 2 * pair + 1]
        keeps[pair] = ((key < first) | ((key >= BLOCK) & (key < second + BLOCK))) & same
        live = (lane < first) | ((lane >= BLOCK) & (lane < second + BLOCK))
        here = slot // 2 == pair
        grad = jnp.where(lent_lanes & here, lent, grad_buf[:, columns].astype(F32))
        grads[pair] = jnp.where(live, grad, 0.0).astype(BF16)
        lives[pair] = live[:HD]
    chains = [(pair, head) for pair in pairs for head in range(2)]

    def part(pair, head, which):
        base = head * 3 * HD + which * HD
        return qkv_buf[base : base + HD, pair * PAIR : (pair + 1) * PAIR]

    q = [part(*c, 0) for c in chains]
    k = [part(*c, 1) for c in chains]
    v = [part(*c, 2) for c in chains]
    g = [grads[pair][head * HD : (head + 1) * HD] for pair, head in chains]
    many = range(len(chains))
    scores = [dot(k[c], q[c], TN) for c in many]
    dp = [dot(v[c], g[c], TN) for c in many]
    scores = [jnp.where(keeps[chains[c][0]], scores[c] * scaling, -1e30) for c in many]
    e = [jnp.exp(s - jnp.max(s, axis=0, keepdims=True)) for s in scores]
    p = [x / jnp.sum(x, axis=0, keepdims=True) for x in e]
    p_half = [x.astype(BF16) for x in p]
    ds = [(p[c] * (dp[c] - jnp.sum(dp[c] * p[c], axis=0, keepdims=True))).astype(BF16) for c in many]
    ctx = [dot(v[c], p_half[c], NN) for c in many]
    dv = [dot(g[c], p_half[c], NT) for c in many]
    dq = [dot(k[c], ds[c], NN) * scaling for c in many]
    dk = [dot(q[c], ds[c], NT) * scaling for c in many]
    for c, (pair, head) in enumerate(chains):
        columns = slice(pair * PAIR, (pair + 1) * PAIR)
        base = head * 3 * HD
        ctx_buf[head * HD : (head + 1) * HD, columns] = jnp.where(lives[pair], ctx[c], 0.0).astype(BF16)
        dqkv_buf[base : base + HD, columns] = dq[c].astype(BF16)
        dqkv_buf[base + HD : base + 2 * HD, columns] = dk[c].astype(BF16)
        dqkv_buf[base + 2 * HD : base + 3 * HD, columns] = dv[c].astype(BF16)


def block_kernel(
    rank_ref, slot_ref, dest_ref, counts_ref, w_ref, x_ref, grad_ref, gathered_ref, ctx_ref, term_ref, dqkv_ref, pack_ref,
    qkv_buf, turned_buf, ctx_buf, dqkv_buf, term_buf, out_sems,
):
    me = rank_ref[0]
    slot = slot_ref[me]
    host = dest_ref[me]
    for start in range(0, D, 256):
        turned_buf[start : start + 256, :] = w_ref[:, start : start + 256].astype(F32).T.astype(BF16)

    def project(group):
        rows = slice(group * STEP, (group + 1) * STEP)
        qkv_buf[:, rows] = dot(w_ref[...], x_ref[rows, :], NT).astype(BF16)

    tile = gathered_ref[pl.ds(pl.multiple_of(lax.rem(host, GROUP) * HD, 16), HD), :]
    upper = lax.rem(slot, 2) == 1
    lent = jnp.concatenate([shifted(tile, upper), shifted(tile, jnp.logical_not(upper))], axis=0)
    for group in range(ROWS // STEP):
        project(group)
    for group in range(ROWS // STEP):
        attend(me, slot, group, lent, counts_ref, grad_ref, qkv_buf, ctx_buf, dqkv_buf)
    stores = [
        pltpu.make_async_copy(ctx_buf, ctx_ref, out_sems.at[0]),
        pltpu.make_async_copy(dqkv_buf, dqkv_ref, out_sems.at[1]),
    ]
    stores[0].start()
    stores[1].start()
    for piece in range(D // CUT):
        rows = pl.ds(piece * CUT, CUT)
        term_buf[rows, :] = dot(turned_buf[rows, :], dqkv_buf[...], NN).astype(BF16)
        stores.append(pltpu.make_async_copy(term_buf.at[rows], term_ref.at[rows], out_sems.at[2 + piece]))
        stores[-1].start()
    mine = ctx_buf[:, pl.ds(pl.multiple_of(slot // 2 * PAIR, PAIR), PAIR)]
    mine = shifted(mine, upper).astype(BF16)
    for piece in range(WIDTH // PACK):
        pack_ref[:, piece * PAIR : (piece + 1) * PAIR] = mine[piece * PACK : (piece + 1) * PACK]
    for store in stores:
        store.wait()


def block(rank, slots, dest, counts, weight, patches, grad, gathered):
    return pl.pallas_call(
        block_kernel,
        in_specs=[SMEM] * 4 + [VMEM] * 4,
        out_specs=[HBM] * 3 + [VMEM],
        out_shape=[
            jax.ShapeDtypeStruct((WIDTH, ROWS), BF16),
            jax.ShapeDtypeStruct((D, ROWS), BF16),
            jax.ShapeDtypeStruct((COLS, ROWS), BF16),
            jax.ShapeDtypeStruct((PACK, D), BF16),
        ],
        scratch_shapes=[
            pltpu.VMEM((COLS, ROWS), BF16),
            pltpu.VMEM((D, COLS), BF16),
            pltpu.VMEM((WIDTH, ROWS), BF16),
            pltpu.VMEM((COLS, ROWS), BF16),
            pltpu.VMEM((D, ROWS), BF16),
            pltpu.SemaphoreType.DMA((2 + D // CUT,)),
        ],
        cost_estimate=pl.CostEstimate(flops=6_000_000_000, bytes_accessed=9_000_000, transcendentals=300_000),
        compiler_params=pltpu.CompilerParams(vmem_limit_bytes=32 * 2**20),
        name="block",
    )(rank, slots, dest, counts, weight, patches, grad, gathered)


def sums_kernel(rank_ref, order_ref, dqkv_ref, x_ref, pack_ref, own_ref, send_ref):
    core = lax.rem(rank_ref[0], 2)
    for which, ref in ((1 - core, send_ref), (core, own_ref)):
        order = order_ref[pl.ds(pl.multiple_of(which * 256, 256), 256), :]
        sorted_grad = dot(order, dqkv_ref[...], NN).astype(BF16)
        ref[0:256, :] = (dot(sorted_grad, x_ref[...], NN) * (1.0 / ROWS)).astype(BF16)
    send_ref[256 : 256 + PACK, :] = pack_ref[...]


def sums(rank, order, dqkv, patches, pack):
    return pl.pallas_call(
        sums_kernel,
        in_specs=[SMEM] + [VMEM] * 4,
        out_specs=[VMEM] * 2,
        out_shape=[jax.ShapeDtypeStruct((256, D), BF16), jax.ShapeDtypeStruct((256 + PACK, D), BF16)],
        cost_estimate=pl.CostEstimate(flops=2_000_000_000, bytes_accessed=6_000_000, transcendentals=0),
        compiler_params=SMALL,
        name="sums",
    )(rank, order, dqkv, patches, pack)


def own_kernel(own_ref, pack_ref, other_ref, out_ref):
    for x in range(N_X):
        rows = slice(64 * x, 64 * (x + 1))
        out_ref[x, 0:64, :] = (own_ref[rows, :].astype(F32) + other_ref[rows, :].astype(F32)).astype(BF16)
    lane = lax.broadcasted_iota(jnp.int32, (PACK, PAIR), 1)
    for piece in range(WIDTH // PACK):
        columns = slice(piece * PAIR, (piece + 1) * PAIR)
        partner = pltpu.roll(other_ref[256 : 256 + PACK, columns].astype(F32), BLOCK, 1)
        both = jnp.where(lane < BLOCK, pack_ref[:, columns].astype(F32), partner).astype(BF16)
        for x in range(N_X):
            out_ref[x, 64 : 64 + PACK, columns] = both


def own_half(own, pack, other):
    return pl.pallas_call(
        own_kernel,
        in_specs=[VMEM] * 3,
        out_specs=VMEM,
        out_shape=jax.ShapeDtypeStruct((N_X, 64 + PACK, D), BF16),
        compiler_params=SMALL,
        name="own_half",
    )(own, pack, other)


def spread_kernel(rank_ref, slot_ref, dest_ref, in_ref, ctx_ref, out_ref, ctx_out_ref, held_ref):
    total = in_ref[0, 0:64, :].astype(F32)
    for x in range(1, N_X):
        total = total + in_ref[x, 0:64, :].astype(F32)
    held_ref[...] = total
    upper = lax.broadcasted_iota(jnp.int32, (8, PAIR), 0) < 5
    for z in range(N_Z):
        rows = held_ref[5 * z : 5 * z + 8, :]
        late = rows[:, WIDE:]
        low, high = pltpu.roll(late, 5, 0), pltpu.roll(late, 2, 0)
        for piece in range(WIDE // PAIR):
            front = rows[:, piece * PAIR : (piece + 1) * PAIR]
            if piece < 6:
                source_piece = (high if piece % 2 else low)[:, piece // 2 * PAIR : (piece // 2 + 1) * PAIR]
                front = jnp.where(upper, front, source_piece)
            out_ref[z, :, piece * PAIR : (piece + 1) * PAIR] = front.astype(BF16)
    me = rank_ref[0]
    base = me // GROUP * GROUP
    source = base
    for k in range(1, GROUP):
        source = jnp.where(dest_ref[base + k] == me, base + k, source)
    slot = slot_ref[me]
    flip = (lax.rem(source, 2) != lax.rem(me, 2)) != (lax.rem(slot, 2) == 1)
    lane = lax.broadcasted_iota(jnp.int32, (PACK, PAIR), 1)
    mine = (lane >= BLOCK) == (lax.rem(slot, 2) == 1)
    x_source = lax.rem(source, 2 * N_X) // 2
    for part in range(WIDTH // PACK):
        rows = slice(part * PACK, (part + 1) * PACK)
        block_in = shifted(in_ref[x_source, 64 : 64 + PACK, part * PAIR : (part + 1) * PAIR], flip)
        ctx_out_ref[rows, :] = jnp.where(mine, block_in, ctx_ref[rows, :].astype(F32)).astype(BF16)


def spread(rank, slots, dest, received, ctx):
    tile = lambda i, rank, slots, dest: (0, slots[rank[0]] // 2)
    return pl.pallas_call(
        spread_kernel,
        grid_spec=pltpu.PrefetchScalarGridSpec(
            num_scalar_prefetch=3,
            grid=(1,),
            in_specs=[
                pl.BlockSpec((N_X, 64 + PACK, D), lambda i, rank, slots, dest: (0, 0, 0)),
                pl.BlockSpec((WIDTH, PAIR), tile),
            ],
            out_specs=[
                pl.BlockSpec((N_Z, 8, WIDE), lambda i, rank, slots, dest: (0, 0, 0)),
                pl.BlockSpec((WIDTH, PAIR), tile),
            ],
            scratch_shapes=[pltpu.VMEM((64, D), F32)],
        ),
        out_shape=[jax.ShapeDtypeStruct((N_Z, 8, WIDE), BF16), jax.ShapeDtypeStruct((WIDTH, ROWS), BF16)],
        input_output_aliases={4: 1},
        compiler_params=SMALL,
        name="spread",
    )(rank, slots, dest, received, ctx)


def last_kernel(in_ref, out_ref):
    total = in_ref[0].astype(F32)
    for z in range(1, N_Z):
        total = total + in_ref[z].astype(F32)
    out_ref[:, 0:WIDE] = total[0:5]
    upper = lax.broadcasted_iota(jnp.int32, (8, PAIR), 0) < 3
    for piece in range(3):
        low = pltpu.roll(total[:, 2 * piece * PAIR : (2 * piece + 1) * PAIR], 3, 0)
        high = pltpu.roll(total[:, (2 * piece + 1) * PAIR : (2 * piece + 2) * PAIR], 6, 0)
        out_ref[:, WIDE + piece * PAIR : WIDE + (piece + 1) * PAIR] = jnp.where(upper, low, high)[0:5]


def last_sum(received):
    return pl.pallas_call(
        last_kernel,
        in_specs=[VMEM],
        out_specs=VMEM,
        out_shape=jax.ShapeDtypeStruct((5, D), F32),
        compiler_params=SMALL,
        name="last_sum",
    )(received)


def shards(patches, qkv_weight, patch_counts, lend_dest, lend_slot, attn_grad):
    rank = lax.axis_index("dp").astype(jnp.int32).reshape(1)
    grad = attn_grad.T
    weight = qkv_weight.T
    groups = [[base + k for k in range(GROUP)] for base in range(0, N_DP, GROUP)]
    x_groups = [[z * 8 + x * 2 + core for x in range(N_X)] for z in range(N_Z) for core in range(2)]
    z_groups = [[z * 8 + place for z in range(N_Z)] for place in range(8)]
    gathered = lax.all_gather(pick(rank, lend_slot, grad), "dp", axis=0, tiled=True, axis_index_groups=groups)
    ctx, terms, dqkv, pack = block(rank, lend_slot, lend_dest, patch_counts, weight, patches, grad, gathered)
    summed = lax.psum_scatter(terms, "tensor", scatter_dimension=0, tiled=True)
    own, sent = sums(rank, jnp.asarray(owner_order()), dqkv, patches, pack)
    received = lax.ppermute(sent, "dp", [(p, p ^ 1) for p in range(N_DP)])
    parts = own_half(own, pack, received)
    parts = lax.all_to_all(parts, "dp", 0, 0, axis_index_groups=x_groups)
    parts, ctx = spread(rank, lend_slot, lend_dest, parts, ctx)
    parts = lax.all_to_all(parts, "dp", 0, 0, axis_index_groups=z_groups)
    return (ctx.T, summed.T, last_sum(parts))


def solution(mesh):
    return jax.shard_map(
        shards,
        mesh=mesh,
        in_specs=(P("dp", None), P(None, "tensor"), P(), P(), P(), P("dp", "tensor")),
        out_specs=(P("dp", "tensor"), P("dp", "tensor"), P(("tensor", "dp"), None)),
        check_vma=False,
    )
```

```python
import jax
import jax.numpy as jnp
from jax import lax
from jax.experimental import pallas as pl
from jax.experimental.pallas import tpu as pltpu
from jax.sharding import PartitionSpec as P

N_DP = 96
IMG_DEV = 16
BLOCK = 64
GROUP = 4
HD = 80
D = 1280
ROWS = 1024
COLS = 480
WIDTH = 2 * HD
PAIR = 2 * BLOCK
STEP = 4 * PAIR
CUT = 256
PARTS = 6
N_X = 4
N_Z = 12
PACK = 16
WIDE = 7 * PAIR
BF16 = jnp.bfloat16
F32 = jnp.float32

NT = (((1,), (1,)), ((), ()))
NN = (((1,), (0,)), ((), ()))
TN = (((0,), (0,)), ((), ()))

VMEM = pl.BlockSpec(memory_space=pltpu.VMEM)
SMEM = pl.BlockSpec(memory_space=pltpu.SMEM)
HBM = pl.BlockSpec(memory_space=pltpu.HBM)
SMALL = pltpu.CompilerParams(vmem_limit_bytes=16 * 2**20)


def owner_order(core):
    row = lax.broadcasted_iota(jnp.int32, (256, COLS), 0)
    column = lax.broadcasted_iota(jnp.int32, (256, COLS), 1)
    place = row & 63
    z = (place * 205) >> 10
    source = z * 35 + place + (row >> 6) * 10 + core * 5
    return jnp.where((source == column) & (place < 5 * N_Z), 1.0, 0.0).astype(BF16)


def dot(a, b, dims):
    return lax.dot_general(a, b, dims, preferred_element_type=F32)


def pick_kernel(rank_ref, slot_ref, in_ref, out_ref):
    upper = lax.rem(slot_ref[rank_ref[0]], 2) == 1
    lane = lax.broadcasted_iota(jnp.int32, (HD, PAIR), 1)
    left = shifted(in_ref[0:HD, :], upper)
    right = shifted(in_ref[HD:WIDTH, :], jnp.logical_not(upper))
    out_ref[...] = jnp.where(lane < BLOCK, left, right).astype(BF16)


def pick(rank, slots, grad):
    return pl.pallas_call(
        pick_kernel,
        grid_spec=pltpu.PrefetchScalarGridSpec(
            num_scalar_prefetch=2,
            grid=(1,),
            in_specs=[pl.BlockSpec((WIDTH, PAIR), lambda i, rank, slots: (0, slots[rank[0]] // 2))],
            out_specs=pl.BlockSpec((HD, PAIR), lambda i, rank, slots: (0, 0)),
        ),
        out_shape=jax.ShapeDtypeStruct((HD, PAIR), BF16),
        cost_estimate=pl.CostEstimate(flops=20_000_000_000, bytes_accessed=40_000_000, transcendentals=0),
        compiler_params=pltpu.CompilerParams(vmem_limit_bytes=60400 * 1024),
        name="pick",
    )(rank, slots, grad)


def shifted(tile, flip):
    wide = tile.astype(F32)
    return jnp.where(flip, pltpu.roll(wide, BLOCK, 1), wide)


def attend(me, slot, group, lent, counts_ref, grad_buf, qkv_buf, ctx_buf, dqkv_buf):
    scaling = HD ** (-0.5)
    lane = lax.broadcasted_iota(jnp.int32, (WIDTH, PAIR), 1)
    lent_lanes = (lane >= BLOCK) == (lax.rem(slot, 2) == 1)
    key = lax.broadcasted_iota(jnp.int32, (PAIR, PAIR), 0)
    query = lax.broadcasted_iota(jnp.int32, (PAIR, PAIR), 1)
    same = (key < BLOCK) == (query < BLOCK)
    pairs = range(group * (STEP // PAIR), (group + 1) * (STEP // PAIR))
    keeps, lives, grads = {}, {}, {}
    for pair in pairs:
        columns = slice(pair * PAIR, (pair + 1) * PAIR)
        first = counts_ref[me * IMG_DEV + 2 * pair]
        second = counts_ref[me * IMG_DEV + 2 * pair + 1]
        keeps[pair] = ((key < first) | ((key >= BLOCK) & (key < second + BLOCK))) & same
        live = (lane < first) | ((lane >= BLOCK) & (lane < second + BLOCK))
        here = slot // 2 == pair
        grad = jnp.where(lent_lanes & here, lent, grad_buf[:, columns].astype(F32))
        grads[pair] = jnp.where(live, grad, 0.0).astype(BF16)
        lives[pair] = live[:HD]
    chains = [(pair, head) for pair in pairs for head in range(2)]

    def part(pair, head, which):
        base = head * 3 * HD + which * HD
        return qkv_buf[base : base + HD, pair * PAIR : (pair + 1) * PAIR]

    q = [part(*c, 0) for c in chains]
    k = [part(*c, 1) for c in chains]
    v = [part(*c, 2) for c in chains]
    g = [grads[pair][head * HD : (head + 1) * HD] for pair, head in chains]
    many = range(len(chains))
    scores = [dot(k[c], q[c], TN) for c in many]
    dp = [dot(v[c], g[c], TN) for c in many]
    scores = [jnp.where(keeps[chains[c][0]], scores[c] * scaling, -1e30) for c in many]
    e = [jnp.exp(s - jnp.max(s, axis=0, keepdims=True)) for s in scores]
    p = [x / jnp.sum(x, axis=0, keepdims=True) for x in e]
    p_half = [x.astype(BF16) for x in p]
    ds = [(p[c] * (dp[c] - jnp.sum(dp[c] * p[c], axis=0, keepdims=True))).astype(BF16) for c in many]
    ctx = [dot(v[c], p_half[c], NN) for c in many]
    dv = [dot(g[c], p_half[c], NT) for c in many]
    dq = [dot(k[c], ds[c], NN) * scaling for c in many]
    dk = [dot(q[c], ds[c], NT) * scaling for c in many]
    for c, (pair, head) in enumerate(chains):
        columns = slice(pair * PAIR, (pair + 1) * PAIR)
        base = head * 3 * HD
        ctx_buf[head * HD : (head + 1) * HD, columns] = jnp.where(lives[pair], ctx[c], 0.0).astype(BF16)
        dqkv_buf[base : base + HD, columns] = dq[c].astype(BF16)
        dqkv_buf[base + HD : base + 2 * HD, columns] = dk[c].astype(BF16)
        dqkv_buf[base + 2 * HD : base + 3 * HD, columns] = dv[c].astype(BF16)


def block_kernel(rank_ref, slot_ref, dest_ref, counts_ref, w_ref, x_ref, grad_ref, gathered_ref, ctx_ref, term_ref, pack_ref, *more):
    dqkv_refs, (qkv_buf, turned_buf, ctx_buf, dqkv_buf, term_buf, out_sems) = more[:PARTS], more[PARTS:]
    me = rank_ref[0]
    slot = slot_ref[me]
    host = dest_ref[me]
    for start in range(0, D, 256):
        turned_buf[start : start + 256, :] = w_ref[:, start : start + 256].astype(F32).T.astype(BF16)

    def project(group):
        rows = slice(group * STEP, (group + 1) * STEP)
        qkv_buf[:, rows] = dot(w_ref[...], x_ref[rows, :], NT).astype(BF16)

    tile = gathered_ref[pl.ds(pl.multiple_of(lax.rem(host, GROUP) * HD, 16), HD), :]
    upper = lax.rem(slot, 2) == 1
    lent = jnp.concatenate([shifted(tile, upper), shifted(tile, jnp.logical_not(upper))], axis=0)
    for group in range(ROWS // STEP):
        project(group)
    for group in range(ROWS // STEP):
        attend(me, slot, group, lent, counts_ref, grad_ref, qkv_buf, ctx_buf, dqkv_buf)
    stores = [pltpu.make_async_copy(ctx_buf, ctx_ref, out_sems.at[0])]
    for part, dqkv_ref in enumerate(dqkv_refs):
        stores.append(pltpu.make_async_copy(dqkv_buf.at[part * HD : (part + 1) * HD], dqkv_ref, out_sems.at[1 + part]))
    for store in stores:
        store.start()
    for piece in range(D // CUT):
        rows = pl.ds(piece * CUT, CUT)
        term_buf[rows, :] = dot(turned_buf[rows, :], dqkv_buf[...], NN).astype(BF16)
        stores.append(pltpu.make_async_copy(term_buf.at[rows], term_ref.at[rows], out_sems.at[1 + PARTS + piece]))
        stores[-1].start()
    mine = ctx_buf[:, pl.ds(pl.multiple_of(slot // 2 * PAIR, PAIR), PAIR)]
    mine = shifted(mine, upper).astype(BF16)
    for piece in range(WIDTH // PACK):
        pack_ref[:, piece * PAIR : (piece + 1) * PAIR] = mine[piece * PACK : (piece + 1) * PACK]
    for store in stores:
        store.wait()


def block(rank, slots, dest, counts, weight, patches, grad, gathered):
    return pl.pallas_call(
        block_kernel,
        in_specs=[SMEM] * 4 + [VMEM] * 4,
        out_specs=[HBM] * 2 + [VMEM] + [HBM] * PARTS,
        out_shape=[
            jax.ShapeDtypeStruct((WIDTH, ROWS), BF16),
            jax.ShapeDtypeStruct((D, ROWS), BF16),
            jax.ShapeDtypeStruct((PACK, D), BF16),
        ]
        + [jax.ShapeDtypeStruct((HD, ROWS), BF16)] * PARTS,
        scratch_shapes=[
            pltpu.VMEM((COLS, ROWS), BF16),
            pltpu.VMEM((D, COLS), BF16),
            pltpu.VMEM((WIDTH, ROWS), BF16),
            pltpu.VMEM((COLS, ROWS), BF16),
            pltpu.VMEM((D, ROWS), BF16),
            pltpu.SemaphoreType.DMA((1 + PARTS + D // CUT,)),
        ],
        cost_estimate=pl.CostEstimate(flops=6_000_000_000, bytes_accessed=9_000_000, transcendentals=300_000),
        compiler_params=pltpu.CompilerParams(vmem_limit_bytes=32 * 2**20),
        name="block",
    )(rank, slots, dest, counts, weight, patches, grad, gathered)


def sums_kernel(rank_ref, x_ref, pack_ref, *more):
    dqkv_refs, (own_ref, send_ref, dqkv_buf) = more[:PARTS], more[PARTS:]
    for part, dqkv_ref in enumerate(dqkv_refs):
        dqkv_buf[part * HD : (part + 1) * HD, :] = dqkv_ref[...]
    core = lax.rem(rank_ref[0], 2)
    for which, ref in ((1 - core, send_ref), (core, own_ref)):
        sorted_grad = dot(owner_order(which), dqkv_buf[...], NN).astype(BF16)
        ref[0:256, :] = (dot(sorted_grad, x_ref[...], NN) * (1.0 / ROWS)).astype(BF16)
    send_ref[256 : 256 + PACK, :] = pack_ref[...]


def sums(rank, patches, pack, dqkv):
    return pl.pallas_call(
        sums_kernel,
        in_specs=[SMEM] + [VMEM] * (2 + PARTS),
        out_specs=[VMEM] * 2,
        out_shape=[jax.ShapeDtypeStruct((256, D), BF16), jax.ShapeDtypeStruct((256 + PACK, D), BF16)],
        scratch_shapes=[pltpu.VMEM((COLS, ROWS), BF16)],
        cost_estimate=pl.CostEstimate(flops=2_000_000_000, bytes_accessed=6_000_000, transcendentals=0),
        compiler_params=SMALL,
        name="sums",
    )(rank, patches, pack, *dqkv)


def own_kernel(own_ref, pack_ref, other_ref, out_ref):
    for x in range(N_X):
        rows = slice(64 * x, 64 * (x + 1))
        out_ref[x, 0:64, :] = (own_ref[rows, :].astype(F32) + other_ref[rows, :].astype(F32)).astype(BF16)
    lane = lax.broadcasted_iota(jnp.int32, (PACK, PAIR), 1)
    for piece in range(WIDTH // PACK):
        columns = slice(piece * PAIR, (piece + 1) * PAIR)
        partner = pltpu.roll(other_ref[256 : 256 + PACK, columns].astype(F32), BLOCK, 1)
        both = jnp.where(lane < BLOCK, pack_ref[:, columns].astype(F32), partner).astype(BF16)
        for x in range(N_X):
            out_ref[x, 64 : 64 + PACK, columns] = both


def own_half(own, pack, other):
    return pl.pallas_call(
        own_kernel,
        in_specs=[VMEM] * 3,
        out_specs=VMEM,
        out_shape=jax.ShapeDtypeStruct((N_X, 64 + PACK, D), BF16),
        compiler_params=SMALL,
        name="own_half",
    )(own, pack, other)


def spread_kernel(rank_ref, slot_ref, dest_ref, in_ref, ctx_ref, out_ref, ctx_out_ref, held_ref):
    total = in_ref[0, 0:64, :].astype(F32)
    for x in range(1, N_X):
        total = total + in_ref[x, 0:64, :].astype(F32)
    held_ref[...] = total
    upper = lax.broadcasted_iota(jnp.int32, (8, PAIR), 0) < 5
    for z in range(N_Z):
        rows = held_ref[5 * z : 5 * z + 8, :]
        late = rows[:, WIDE:]
        low, high = pltpu.roll(late, 5, 0), pltpu.roll(late, 2, 0)
        for piece in range(WIDE // PAIR):
            front = rows[:, piece * PAIR : (piece + 1) * PAIR]
            if piece < 6:
                source_piece = (high if piece % 2 else low)[:, piece // 2 * PAIR : (piece // 2 + 1) * PAIR]
                front = jnp.where(upper, front, source_piece)
            out_ref[z, :, piece * PAIR : (piece + 1) * PAIR] = front.astype(BF16)
    me = rank_ref[0]
    base = me // GROUP * GROUP
    source = base
    for k in range(1, GROUP):
        source = jnp.where(dest_ref[base + k] == me, base + k, source)
    slot = slot_ref[me]
    flip = (lax.rem(source, 2) != lax.rem(me, 2)) != (lax.rem(slot, 2) == 1)
    lane = lax.broadcasted_iota(jnp.int32, (PACK, PAIR), 1)
    mine = (lane >= BLOCK) == (lax.rem(slot, 2) == 1)
    x_source = lax.rem(source, 2 * N_X) // 2
    for part in range(WIDTH // PACK):
        rows = slice(part * PACK, (part + 1) * PACK)
        block_in = shifted(in_ref[x_source, 64 : 64 + PACK, part * PAIR : (part + 1) * PAIR], flip)
        ctx_out_ref[rows, :] = jnp.where(mine, block_in, ctx_ref[rows, :].astype(F32)).astype(BF16)


def spread(rank, slots, dest, received, ctx):
    tile = lambda i, rank, slots, dest: (0, slots[rank[0]] // 2)
    return pl.pallas_call(
        spread_kernel,
        grid_spec=pltpu.PrefetchScalarGridSpec(
            num_scalar_prefetch=3,
            grid=(1,),
            in_specs=[
                pl.BlockSpec((N_X, 64 + PACK, D), lambda i, rank, slots, dest: (0, 0, 0)),
                pl.BlockSpec((WIDTH, PAIR), tile),
            ],
            out_specs=[
                pl.BlockSpec((N_Z, 8, WIDE), lambda i, rank, slots, dest: (0, 0, 0)),
                pl.BlockSpec((WIDTH, PAIR), tile),
            ],
            scratch_shapes=[pltpu.VMEM((64, D), F32)],
        ),
        out_shape=[jax.ShapeDtypeStruct((N_Z, 8, WIDE), BF16), jax.ShapeDtypeStruct((WIDTH, ROWS), BF16)],
        input_output_aliases={4: 1},
        compiler_params=SMALL,
        name="spread",
    )(rank, slots, dest, received, ctx)


def last_kernel(in_ref, out_ref):
    total = in_ref[0].astype(F32)
    for z in range(1, N_Z):
        total = total + in_ref[z].astype(F32)
    out_ref[:, 0:WIDE] = total[0:5]
    upper = lax.broadcasted_iota(jnp.int32, (8, PAIR), 0) < 3
    for piece in range(3):
        low = pltpu.roll(total[:, 2 * piece * PAIR : (2 * piece + 1) * PAIR], 3, 0)
        high = pltpu.roll(total[:, (2 * piece + 1) * PAIR : (2 * piece + 2) * PAIR], 6, 0)
        out_ref[:, WIDE + piece * PAIR : WIDE + (piece + 1) * PAIR] = jnp.where(upper, low, high)[0:5]


def last_sum(received):
    return pl.pallas_call(
        last_kernel,
        in_specs=[VMEM],
        out_specs=VMEM,
        out_shape=jax.ShapeDtypeStruct((5, D), F32),
        compiler_params=SMALL,
        name="last_sum",
    )(received)


def shards(patches, qkv_weight, patch_counts, lend_dest, lend_slot, attn_grad):
    rank = lax.axis_index("dp").astype(jnp.int32).reshape(1)
    grad = attn_grad.T
    weight = qkv_weight.T
    groups = [[base + k for k in range(GROUP)] for base in range(0, N_DP, GROUP)]
    x_groups = [[z * 8 + x * 2 + core for x in range(N_X)] for z in range(N_Z) for core in range(2)]
    z_groups = [[z * 8 + place for z in range(N_Z)] for place in range(8)]
    gathered = lax.all_gather(pick(rank, lend_slot, grad), "dp", axis=0, tiled=True, axis_index_groups=groups)
    ctx, terms, pack, *dqkv = block(rank, lend_slot, lend_dest, patch_counts, weight, patches, grad, gathered)
    summed = lax.psum_scatter(terms, "tensor", scatter_dimension=0, tiled=True)
    own, sent = sums(rank, patches, pack, dqkv)
    received = lax.ppermute(sent, "dp", [(p, p ^ 1) for p in range(N_DP)])
    parts = own_half(own, pack, received)
    parts = lax.all_to_all(parts, "dp", 0, 0, axis_index_groups=x_groups)
    parts, ctx = spread(rank, lend_slot, lend_dest, parts, ctx)
    parts = lax.all_to_all(parts, "dp", 0, 0, axis_index_groups=z_groups)
    return (ctx.T, summed.T, last_sum(parts))


def solution(mesh):
    return jax.shard_map(
        shards,
        mesh=mesh,
        in_specs=(P("dp", None), P(None, "tensor"), P(), P(), P(), P("dp", "tensor")),
        out_specs=(P("dp", "tensor"), P("dp", "tensor"), P(("tensor", "dp"), None)),
        check_vma=False,
    )
```

```python
import jax
import jax.numpy as jnp
from jax import lax
from jax.experimental import pallas as pl
from jax.experimental.pallas import tpu as pltpu
from jax.sharding import PartitionSpec as P

N_DP = 96
IMG_DEV = 16
BLOCK = 64
GROUP = 4
HD = 80
D = 1280
ROWS = 1024
COLS = 480
WIDTH = 2 * HD
PAIR = 2 * BLOCK
STEP = 4 * PAIR
CUT = 256
PARTS = 6
N_X = 4
N_Z = 12
PACK = 16
WIDE = 7 * PAIR
BF16 = jnp.bfloat16
F32 = jnp.float32

NT = (((1,), (1,)), ((), ()))
NN = (((1,), (0,)), ((), ()))
TN = (((0,), (0,)), ((), ()))

VMEM = pl.BlockSpec(memory_space=pltpu.VMEM)
SMEM = pl.BlockSpec(memory_space=pltpu.SMEM)
HBM = pl.BlockSpec(memory_space=pltpu.HBM)
SMALL = pltpu.CompilerParams(vmem_limit_bytes=16 * 2**20)


def owner_order(core):
    row = lax.broadcasted_iota(jnp.int32, (256, COLS), 0)
    column = lax.broadcasted_iota(jnp.int32, (256, COLS), 1)
    place = row & 63
    z = (place * 205) >> 10
    source = z * 35 + place + (row >> 6) * 10 + core * 5
    return jnp.where((source == column) & (place < 5 * N_Z), 1.0, 0.0).astype(BF16)


def dot(a, b, dims):
    return lax.dot_general(a, b, dims, preferred_element_type=F32)


def pick_kernel(rank_ref, slot_ref, in_ref, out_ref):
    upper = lax.rem(slot_ref[rank_ref[0]], 2) == 1
    lane = lax.broadcasted_iota(jnp.int32, (HD, PAIR), 1)
    left = shifted(in_ref[0:HD, :], upper)
    right = shifted(in_ref[HD:WIDTH, :], jnp.logical_not(upper))
    out_ref[...] = jnp.where(lane < BLOCK, left, right).astype(BF16)


def pick(rank, slots, grad):
    return pl.pallas_call(
        pick_kernel,
        grid_spec=pltpu.PrefetchScalarGridSpec(
            num_scalar_prefetch=2,
            grid=(1,),
            in_specs=[pl.BlockSpec((WIDTH, PAIR), lambda i, rank, slots: (0, slots[rank[0]] // 2))],
            out_specs=pl.BlockSpec((HD, PAIR), lambda i, rank, slots: (0, 0)),
        ),
        out_shape=jax.ShapeDtypeStruct((HD, PAIR), BF16),
        cost_estimate=pl.CostEstimate(flops=20_000_000_000, bytes_accessed=40_000_000, transcendentals=0),
        compiler_params=pltpu.CompilerParams(vmem_limit_bytes=60400 * 1024),
        name="pick",
    )(rank, slots, grad)


def shifted(tile, flip):
    wide = tile.astype(F32)
    return jnp.where(flip, pltpu.roll(wide, BLOCK, 1), wide)


def attend(me, slot, group, lent, counts_ref, grad_buf, qkv_buf, ctx_buf, dqkv_buf):
    scaling = HD ** (-0.5)
    lane = lax.broadcasted_iota(jnp.int32, (WIDTH, PAIR), 1)
    lent_lanes = (lane >= BLOCK) == (lax.rem(slot, 2) == 1)
    key = lax.broadcasted_iota(jnp.int32, (PAIR, PAIR), 0)
    query = lax.broadcasted_iota(jnp.int32, (PAIR, PAIR), 1)
    same = (key < BLOCK) == (query < BLOCK)
    pairs = range(group * (STEP // PAIR), (group + 1) * (STEP // PAIR))
    keeps, lives, grads = {}, {}, {}
    for pair in pairs:
        columns = slice(pair * PAIR, (pair + 1) * PAIR)
        first = counts_ref[me * IMG_DEV + 2 * pair]
        second = counts_ref[me * IMG_DEV + 2 * pair + 1]
        keeps[pair] = ((key < first) | ((key >= BLOCK) & (key < second + BLOCK))) & same
        live = (lane < first) | ((lane >= BLOCK) & (lane < second + BLOCK))
        here = slot // 2 == pair
        grad = jnp.where(lent_lanes & here, lent, grad_buf[:, columns].astype(F32))
        grads[pair] = jnp.where(live, grad, 0.0).astype(BF16)
        lives[pair] = live[:HD]
    chains = [(pair, head) for pair in pairs for head in range(2)]

    def part(pair, head, which):
        base = head * 3 * HD + which * HD
        return qkv_buf[base : base + HD, pair * PAIR : (pair + 1) * PAIR]

    q = [part(*c, 0) for c in chains]
    k = [part(*c, 1) for c in chains]
    v = [part(*c, 2) for c in chains]
    g = [grads[pair][head * HD : (head + 1) * HD] for pair, head in chains]
    many = range(len(chains))
    scores = [dot(k[c], q[c], TN) for c in many]
    dp = [dot(v[c], g[c], TN) for c in many]
    scores = [jnp.where(keeps[chains[c][0]], scores[c] * scaling, -1e30) for c in many]
    e = [jnp.exp(s - jnp.max(s, axis=0, keepdims=True)) for s in scores]
    p = [x / jnp.sum(x, axis=0, keepdims=True) for x in e]
    p_half = [x.astype(BF16) for x in p]
    ds = [(p[c] * (dp[c] - jnp.sum(dp[c] * p[c], axis=0, keepdims=True))).astype(BF16) for c in many]
    ctx = [dot(v[c], p_half[c], NN) for c in many]
    dv = [dot(g[c], p_half[c], NT) for c in many]
    dq = [dot(k[c], ds[c], NN) * scaling for c in many]
    dk = [dot(q[c], ds[c], NT) * scaling for c in many]
    for c, (pair, head) in enumerate(chains):
        columns = slice(pair * PAIR, (pair + 1) * PAIR)
        base = head * 3 * HD
        ctx_buf[head * HD : (head + 1) * HD, columns] = jnp.where(lives[pair], ctx[c], 0.0).astype(BF16)
        dqkv_buf[base : base + HD, columns] = dq[c].astype(BF16)
        dqkv_buf[base + HD : base + 2 * HD, columns] = dk[c].astype(BF16)
        dqkv_buf[base + 2 * HD : base + 3 * HD, columns] = dv[c].astype(BF16)


def block_kernel(rank_ref, slot_ref, dest_ref, counts_ref, w_ref, x_ref, grad_ref, gathered_ref, ctx_ref, term_ref, pack_ref, *more):
    dqkv_refs, (qkv_buf, turned_buf, ctx_buf, dqkv_buf, term_buf, out_sems) = more[:PARTS], more[PARTS:]
    me = rank_ref[0]
    slot = slot_ref[me]
    host = dest_ref[me]
    for start in range(0, D, 256):
        turned_buf[start : start + 256, :] = w_ref[:, start : start + 256].astype(F32).T.astype(BF16)

    def project(group):
        rows = slice(group * STEP, (group + 1) * STEP)
        qkv_buf[:, rows] = dot(w_ref[...], x_ref[rows, :], NT).astype(BF16)

    tile = gathered_ref[pl.ds(pl.multiple_of(lax.rem(host, GROUP) * HD, 16), HD), :]
    upper = lax.rem(slot, 2) == 1
    lent = jnp.concatenate([shifted(tile, upper), shifted(tile, jnp.logical_not(upper))], axis=0)
    for group in range(ROWS // STEP):
        project(group)
    for group in range(ROWS // STEP):
        attend(me, slot, group, lent, counts_ref, grad_ref, qkv_buf, ctx_buf, dqkv_buf)
    stores = [pltpu.make_async_copy(ctx_buf, ctx_ref, out_sems.at[0])]
    for part, dqkv_ref in enumerate(dqkv_refs):
        dqkv_ref[...] = dqkv_buf[part * HD : (part + 1) * HD, :]
    for store in stores:
        store.start()
    for piece in range(D // CUT):
        rows = pl.ds(piece * CUT, CUT)
        term_buf[rows, :] = dot(turned_buf[rows, :], dqkv_buf[...], NN).astype(BF16)
        stores.append(pltpu.make_async_copy(term_buf.at[rows], term_ref.at[rows], out_sems.at[1 + piece]))
        stores[-1].start()
    mine = ctx_buf[:, pl.ds(pl.multiple_of(slot // 2 * PAIR, PAIR), PAIR)]
    mine = shifted(mine, upper).astype(BF16)
    for piece in range(WIDTH // PACK):
        pack_ref[:, piece * PAIR : (piece + 1) * PAIR] = mine[piece * PACK : (piece + 1) * PACK]
    for store in stores:
        store.wait()


def block(rank, slots, dest, counts, weight, patches, grad, gathered):
    return pl.pallas_call(
        block_kernel,
        in_specs=[SMEM] * 4 + [VMEM] * 4,
        out_specs=[HBM] * 2 + [VMEM] * (1 + PARTS),
        out_shape=[
            jax.ShapeDtypeStruct((WIDTH, ROWS), BF16),
            jax.ShapeDtypeStruct((D, ROWS), BF16),
            jax.ShapeDtypeStruct((PACK, D), BF16),
        ]
        + [jax.ShapeDtypeStruct((HD, ROWS), BF16)] * PARTS,
        scratch_shapes=[
            pltpu.VMEM((COLS, ROWS), BF16),
            pltpu.VMEM((D, COLS), BF16),
            pltpu.VMEM((WIDTH, ROWS), BF16),
            pltpu.VMEM((COLS, ROWS), BF16),
            pltpu.VMEM((D, ROWS), BF16),
            pltpu.SemaphoreType.DMA((1 + D // CUT,)),
        ],
        cost_estimate=pl.CostEstimate(flops=6_000_000_000, bytes_accessed=9_000_000, transcendentals=300_000),
        compiler_params=pltpu.CompilerParams(vmem_limit_bytes=32 * 2**20),
        name="block",
    )(rank, slots, dest, counts, weight, patches, grad, gathered)


def sums_kernel(rank_ref, x_ref, pack_ref, *more):
    dqkv_refs, (own_ref, send_ref, dqkv_buf) = more[:PARTS], more[PARTS:]
    for part, dqkv_ref in enumerate(dqkv_refs):
        dqkv_buf[part * HD : (part + 1) * HD, :] = dqkv_ref[...]
    core = lax.rem(rank_ref[0], 2)
    for which, ref in ((1 - core, send_ref), (core, own_ref)):
        sorted_grad = dot(owner_order(which), dqkv_buf[...], NN).astype(BF16)
        ref[0:256, :] = (dot(sorted_grad, x_ref[...], NN) * (1.0 / ROWS)).astype(BF16)
    send_ref[256 : 256 + PACK, :] = pack_ref[...]


def sums(rank, patches, pack, dqkv):
    return pl.pallas_call(
        sums_kernel,
        in_specs=[SMEM] + [VMEM] * (2 + PARTS),
        out_specs=[VMEM] * 2,
        out_shape=[jax.ShapeDtypeStruct((256, D), BF16), jax.ShapeDtypeStruct((256 + PACK, D), BF16)],
        scratch_shapes=[pltpu.VMEM((COLS, ROWS), BF16)],
        cost_estimate=pl.CostEstimate(flops=2_000_000_000, bytes_accessed=6_000_000, transcendentals=0),
        compiler_params=SMALL,
        name="sums",
    )(rank, patches, pack, *dqkv)


def own_kernel(own_ref, pack_ref, other_ref, out_ref):
    for x in range(N_X):
        rows = slice(64 * x, 64 * (x + 1))
        out_ref[x, 0:64, :] = (own_ref[rows, :].astype(F32) + other_ref[rows, :].astype(F32)).astype(BF16)
    lane = lax.broadcasted_iota(jnp.int32, (PACK, PAIR), 1)
    for piece in range(WIDTH // PACK):
        columns = slice(piece * PAIR, (piece + 1) * PAIR)
        partner = pltpu.roll(other_ref[256 : 256 + PACK, columns].astype(F32), BLOCK, 1)
        both = jnp.where(lane < BLOCK, pack_ref[:, columns].astype(F32), partner).astype(BF16)
        for x in range(N_X):
            out_ref[x, 64 : 64 + PACK, columns] = both


def own_half(own, pack, other):
    return pl.pallas_call(
        own_kernel,
        in_specs=[VMEM] * 3,
        out_specs=VMEM,
        out_shape=jax.ShapeDtypeStruct((N_X, 64 + PACK, D), BF16),
        compiler_params=SMALL,
        name="own_half",
    )(own, pack, other)


def spread_kernel(rank_ref, slot_ref, dest_ref, in_ref, ctx_ref, out_ref, ctx_out_ref, held_ref):
    total = in_ref[0, 0:64, :].astype(F32)
    for x in range(1, N_X):
        total = total + in_ref[x, 0:64, :].astype(F32)
    held_ref[...] = total
    upper = lax.broadcasted_iota(jnp.int32, (8, PAIR), 0) < 5
    for z in range(N_Z):
        rows = held_ref[5 * z : 5 * z + 8, :]
        late = rows[:, WIDE:]
        low, high = pltpu.roll(late, 5, 0), pltpu.roll(late, 2, 0)
        for piece in range(WIDE // PAIR):
            front = rows[:, piece * PAIR : (piece + 1) * PAIR]
            if piece < 6:
                source_piece = (high if piece % 2 else low)[:, piece // 2 * PAIR : (piece // 2 + 1) * PAIR]
                front = jnp.where(upper, front, source_piece)
            out_ref[z, :, piece * PAIR : (piece + 1) * PAIR] = front.astype(BF16)
    me = rank_ref[0]
    base = me // GROUP * GROUP
    source = base
    for k in range(1, GROUP):
        source = jnp.where(dest_ref[base + k] == me, base + k, source)
    slot = slot_ref[me]
    flip = (lax.rem(source, 2) != lax.rem(me, 2)) != (lax.rem(slot, 2) == 1)
    lane = lax.broadcasted_iota(jnp.int32, (PACK, PAIR), 1)
    mine = (lane >= BLOCK) == (lax.rem(slot, 2) == 1)
    x_source = lax.rem(source, 2 * N_X) // 2
    for part in range(WIDTH // PACK):
        rows = slice(part * PACK, (part + 1) * PACK)
        block_in = shifted(in_ref[x_source, 64 : 64 + PACK, part * PAIR : (part + 1) * PAIR], flip)
        ctx_out_ref[rows, :] = jnp.where(mine, block_in, ctx_ref[rows, :].astype(F32)).astype(BF16)


def spread(rank, slots, dest, received, ctx):
    tile = lambda i, rank, slots, dest: (0, slots[rank[0]] // 2)
    return pl.pallas_call(
        spread_kernel,
        grid_spec=pltpu.PrefetchScalarGridSpec(
            num_scalar_prefetch=3,
            grid=(1,),
            in_specs=[
                pl.BlockSpec((N_X, 64 + PACK, D), lambda i, rank, slots, dest: (0, 0, 0)),
                pl.BlockSpec((WIDTH, PAIR), tile),
            ],
            out_specs=[
                pl.BlockSpec((N_Z, 8, WIDE), lambda i, rank, slots, dest: (0, 0, 0)),
                pl.BlockSpec((WIDTH, PAIR), tile),
            ],
            scratch_shapes=[pltpu.VMEM((64, D), F32)],
        ),
        out_shape=[jax.ShapeDtypeStruct((N_Z, 8, WIDE), BF16), jax.ShapeDtypeStruct((WIDTH, ROWS), BF16)],
        input_output_aliases={4: 1},
        compiler_params=SMALL,
        name="spread",
    )(rank, slots, dest, received, ctx)


def last_kernel(in_ref, out_ref):
    total = in_ref[0].astype(F32)
    for z in range(1, N_Z):
        total = total + in_ref[z].astype(F32)
    out_ref[:, 0:WIDE] = total[0:5]
    upper = lax.broadcasted_iota(jnp.int32, (8, PAIR), 0) < 3
    for piece in range(3):
        low = pltpu.roll(total[:, 2 * piece * PAIR : (2 * piece + 1) * PAIR], 3, 0)
        high = pltpu.roll(total[:, (2 * piece + 1) * PAIR : (2 * piece + 2) * PAIR], 6, 0)
        out_ref[:, WIDE + piece * PAIR : WIDE + (piece + 1) * PAIR] = jnp.where(upper, low, high)[0:5]


def last_sum(received):
    return pl.pallas_call(
        last_kernel,
        in_specs=[VMEM],
        out_specs=VMEM,
        out_shape=jax.ShapeDtypeStruct((5, D), F32),
        compiler_params=SMALL,
        name="last_sum",
    )(received)


def shards(patches, qkv_weight, patch_counts, lend_dest, lend_slot, attn_grad):
    rank = lax.axis_index("dp").astype(jnp.int32).reshape(1)
    grad = attn_grad.T
    weight = qkv_weight.T
    groups = [[base + k for k in range(GROUP)] for base in range(0, N_DP, GROUP)]
    x_groups = [[z * 8 + x * 2 + core for x in range(N_X)] for z in range(N_Z) for core in range(2)]
    z_groups = [[z * 8 + place for z in range(N_Z)] for place in range(8)]
    gathered = lax.all_gather(pick(rank, lend_slot, grad), "dp", axis=0, tiled=True, axis_index_groups=groups)
    ctx, terms, pack, *dqkv = block(rank, lend_slot, lend_dest, patch_counts, weight, patches, grad, gathered)
    summed = lax.psum_scatter(terms, "tensor", scatter_dimension=0, tiled=True)
    own, sent = sums(rank, patches, pack, dqkv)
    received = lax.ppermute(sent, "dp", [(p, p ^ 1) for p in range(N_DP)])
    parts = own_half(own, pack, received)
    parts = lax.all_to_all(parts, "dp", 0, 0, axis_index_groups=x_groups)
    parts, ctx = spread(rank, lend_slot, lend_dest, parts, ctx)
    parts = lax.all_to_all(parts, "dp", 0, 0, axis_index_groups=z_groups)
    return (ctx.T, summed.T, last_sum(parts))


def solution(mesh):
    return jax.shard_map(
        shards,
        mesh=mesh,
        in_specs=(P("dp", None), P(None, "tensor"), P(), P(), P(), P("dp", "tensor")),
        out_specs=(P("dp", "tensor"), P("dp", "tensor"), P(("tensor", "dp"), None)),
        check_vma=False,
    )
```

```python
import jax
import jax.numpy as jnp
from jax import lax
from jax.experimental import pallas as pl
from jax.experimental.pallas import tpu as pltpu
from jax.sharding import PartitionSpec as P

N_DP = 96
IMG_DEV = 16
BLOCK = 64
GROUP = 4
HD = 80
D = 1280
ROWS = 1024
COLS = 480
WIDTH = 2 * HD
PAIR = 2 * BLOCK
STEP = 4 * PAIR
CUT = 256
PARTS = 6
N_X = 4
N_Z = 12
PACK = 16
WIDE = 7 * PAIR
BF16 = jnp.bfloat16
F32 = jnp.float32

NT = (((1,), (1,)), ((), ()))
NN = (((1,), (0,)), ((), ()))
TN = (((0,), (0,)), ((), ()))

VMEM = pl.BlockSpec(memory_space=pltpu.VMEM)
SMEM = pl.BlockSpec(memory_space=pltpu.SMEM)
HBM = pl.BlockSpec(memory_space=pltpu.HBM)
SMALL = pltpu.CompilerParams(vmem_limit_bytes=16 * 2**20)


def owner_order(core):
    row = lax.broadcasted_iota(jnp.int32, (256, COLS), 0)
    column = lax.broadcasted_iota(jnp.int32, (256, COLS), 1)
    place = row & 63
    z = (place * 205) >> 10
    source = z * 35 + place + (row >> 6) * 10 + core * 5
    return jnp.where((source == column) & (place < 5 * N_Z), 1.0, 0.0).astype(BF16)


def dot(a, b, dims):
    return lax.dot_general(a, b, dims, preferred_element_type=F32)


def pick_kernel(slot_ref, in_ref, out_ref, tile_ref, sem):
    slot = slot_ref[lax.axis_index("dp")]
    copy = pltpu.make_async_copy(in_ref.at[:, pl.ds(pl.multiple_of(slot // 2 * PAIR, PAIR), PAIR)], tile_ref, sem)
    copy.start()
    copy.wait()
    upper = lax.rem(slot, 2) == 1
    lane = lax.broadcasted_iota(jnp.int32, (HD, PAIR), 1)
    left = shifted(tile_ref[0:HD, :], upper)
    right = shifted(tile_ref[HD:WIDTH, :], jnp.logical_not(upper))
    out_ref[...] = jnp.where(lane < BLOCK, left, right).astype(BF16)


def pick(slots, grad):
    return pl.pallas_call(
        pick_kernel,
        in_specs=[SMEM, HBM],
        out_specs=VMEM,
        out_shape=jax.ShapeDtypeStruct((HD, PAIR), BF16),
        scratch_shapes=[pltpu.VMEM((WIDTH, PAIR), BF16), pltpu.SemaphoreType.DMA],
        cost_estimate=pl.CostEstimate(flops=20_000_000_000, bytes_accessed=40_000_000, transcendentals=0),
        compiler_params=pltpu.CompilerParams(vmem_limit_bytes=60400 * 1024),
        name="pick",
    )(slots, grad)


def shifted(tile, flip):
    wide = tile.astype(F32)
    return jnp.where(flip, pltpu.roll(wide, BLOCK, 1), wide)


def attend(me, slot, group, lent, counts_ref, grad_buf, qkv_buf, ctx_buf, dqkv_buf):
    scaling = HD ** (-0.5)
    lane = lax.broadcasted_iota(jnp.int32, (WIDTH, PAIR), 1)
    lent_lanes = (lane >= BLOCK) == (lax.rem(slot, 2) == 1)
    key = lax.broadcasted_iota(jnp.int32, (PAIR, PAIR), 0)
    query = lax.broadcasted_iota(jnp.int32, (PAIR, PAIR), 1)
    same = (key < BLOCK) == (query < BLOCK)
    pairs = range(group * (STEP // PAIR), (group + 1) * (STEP // PAIR))
    keeps, lives, grads = {}, {}, {}
    for pair in pairs:
        columns = slice(pair * PAIR, (pair + 1) * PAIR)
        first = counts_ref[me * IMG_DEV + 2 * pair]
        second = counts_ref[me * IMG_DEV + 2 * pair + 1]
        keeps[pair] = ((key < first) | ((key >= BLOCK) & (key < second + BLOCK))) & same
        live = (lane < first) | ((lane >= BLOCK) & (lane < second + BLOCK))
        here = slot // 2 == pair
        grad = jnp.where(lent_lanes & here, lent, grad_buf[:, columns].astype(F32))
        grads[pair] = jnp.where(live, grad, 0.0).astype(BF16)
        lives[pair] = live[:HD]
    chains = [(pair, head) for pair in pairs for head in range(2)]

    def part(pair, head, which):
        base = head * 3 * HD + which * HD
        return qkv_buf[base : base + HD, pair * PAIR : (pair + 1) * PAIR]

    q = [part(*c, 0) for c in chains]
    k = [part(*c, 1) for c in chains]
    v = [part(*c, 2) for c in chains]
    g = [grads[pair][head * HD : (head + 1) * HD] for pair, head in chains]
    many = range(len(chains))
    scores = [dot(k[c], q[c], TN) for c in many]
    dp = [dot(v[c], g[c], TN) for c in many]
    scores = [jnp.where(keeps[chains[c][0]], scores[c] * scaling, -1e30) for c in many]
    e = [jnp.exp(s - jnp.max(s, axis=0, keepdims=True)) for s in scores]
    p = [x / jnp.sum(x, axis=0, keepdims=True) for x in e]
    p_half = [x.astype(BF16) for x in p]
    ds = [(p[c] * (dp[c] - jnp.sum(dp[c] * p[c], axis=0, keepdims=True))).astype(BF16) for c in many]
    ctx = [dot(v[c], p_half[c], NN) for c in many]
    dv = [dot(g[c], p_half[c], NT) for c in many]
    dq = [dot(k[c], ds[c], NN) * scaling for c in many]
    dk = [dot(q[c], ds[c], NT) * scaling for c in many]
    for c, (pair, head) in enumerate(chains):
        columns = slice(pair * PAIR, (pair + 1) * PAIR)
        base = head * 3 * HD
        ctx_buf[head * HD : (head + 1) * HD, columns] = jnp.where(lives[pair], ctx[c], 0.0).astype(BF16)
        dqkv_buf[base : base + HD, columns] = dq[c].astype(BF16)
        dqkv_buf[base + HD : base + 2 * HD, columns] = dk[c].astype(BF16)
        dqkv_buf[base + 2 * HD : base + 3 * HD, columns] = dv[c].astype(BF16)


def block_kernel(rank_ref, slot_ref, dest_ref, counts_ref, w_ref, x_ref, grad_ref, gathered_ref, ctx_ref, term_ref, pack_ref, *more):
    dqkv_refs, (qkv_buf, turned_buf, ctx_buf, dqkv_buf, term_buf, out_sems) = more[:PARTS], more[PARTS:]
    me = rank_ref[0]
    slot = slot_ref[me]
    host = dest_ref[me]
    for start in range(0, D, 256):
        turned_buf[start : start + 256, :] = w_ref[:, start : start + 256].astype(F32).T.astype(BF16)

    def project(group):
        rows = slice(group * STEP, (group + 1) * STEP)
        qkv_buf[:, rows] = dot(w_ref[...], x_ref[rows, :], NT).astype(BF16)

    tile = gathered_ref[pl.ds(pl.multiple_of(lax.rem(host, GROUP) * HD, 16), HD), :]
    upper = lax.rem(slot, 2) == 1
    lent = jnp.concatenate([shifted(tile, upper), shifted(tile, jnp.logical_not(upper))], axis=0)
    for group in range(ROWS // STEP):
        project(group)
    for group in range(ROWS // STEP):
        attend(me, slot, group, lent, counts_ref, grad_ref, qkv_buf, ctx_buf, dqkv_buf)
    stores = [pltpu.make_async_copy(ctx_buf, ctx_ref, out_sems.at[0])]
    for part, dqkv_ref in enumerate(dqkv_refs):
        dqkv_ref[...] = dqkv_buf[part * HD : (part + 1) * HD, :]
    for store in stores:
        store.start()
    for piece in range(D // CUT):
        rows = pl.ds(piece * CUT, CUT)
        term_buf[rows, :] = dot(turned_buf[rows, :], dqkv_buf[...], NN).astype(BF16)
        stores.append(pltpu.make_async_copy(term_buf.at[rows], term_ref.at[rows], out_sems.at[1 + piece]))
        stores[-1].start()
    mine = ctx_buf[:, pl.ds(pl.multiple_of(slot // 2 * PAIR, PAIR), PAIR)]
    mine = shifted(mine, upper).astype(BF16)
    for piece in range(WIDTH // PACK):
        pack_ref[:, piece * PAIR : (piece + 1) * PAIR] = mine[piece * PACK : (piece + 1) * PACK]
    for store in stores:
        store.wait()


def block(rank, slots, dest, counts, weight, patches, grad, gathered):
    return pl.pallas_call(
        block_kernel,
        in_specs=[SMEM] * 4 + [VMEM] * 4,
        out_specs=[HBM] * 2 + [VMEM] * (1 + PARTS),
        out_shape=[
            jax.ShapeDtypeStruct((WIDTH, ROWS), BF16),
            jax.ShapeDtypeStruct((D, ROWS), BF16),
            jax.ShapeDtypeStruct((PACK, D), BF16),
        ]
        + [jax.ShapeDtypeStruct((HD, ROWS), BF16)] * PARTS,
        scratch_shapes=[
            pltpu.VMEM((COLS, ROWS), BF16),
            pltpu.VMEM((D, COLS), BF16),
            pltpu.VMEM((WIDTH, ROWS), BF16),
            pltpu.VMEM((COLS, ROWS), BF16),
            pltpu.VMEM((D, ROWS), BF16),
            pltpu.SemaphoreType.DMA((1 + D // CUT,)),
        ],
        cost_estimate=pl.CostEstimate(flops=6_000_000_000, bytes_accessed=9_000_000, transcendentals=300_000),
        compiler_params=pltpu.CompilerParams(vmem_limit_bytes=32 * 2**20),
        name="block",
    )(rank, slots, dest, counts, weight, patches, grad, gathered)


def sums_kernel(rank_ref, x_ref, pack_ref, *more):
    dqkv_refs, (own_ref, send_ref, dqkv_buf) = more[:PARTS], more[PARTS:]
    for part, dqkv_ref in enumerate(dqkv_refs):
        dqkv_buf[part * HD : (part + 1) * HD, :] = dqkv_ref[...]
    core = lax.rem(rank_ref[0], 2)
    for which, ref in ((1 - core, send_ref), (core, own_ref)):
        sorted_grad = dot(owner_order(which), dqkv_buf[...], NN).astype(BF16)
        ref[0:256, :] = (dot(sorted_grad, x_ref[...], NN) * (1.0 / ROWS)).astype(BF16)
    send_ref[256 : 256 + PACK, :] = pack_ref[...]


def sums(rank, patches, pack, dqkv):
    return pl.pallas_call(
        sums_kernel,
        in_specs=[SMEM] + [VMEM] * (2 + PARTS),
        out_specs=[VMEM] * 2,
        out_shape=[jax.ShapeDtypeStruct((256, D), BF16), jax.ShapeDtypeStruct((256 + PACK, D), BF16)],
        scratch_shapes=[pltpu.VMEM((COLS, ROWS), BF16)],
        cost_estimate=pl.CostEstimate(flops=2_000_000_000, bytes_accessed=6_000_000, transcendentals=0),
        compiler_params=SMALL,
        name="sums",
    )(rank, patches, pack, *dqkv)


def own_kernel(own_ref, pack_ref, other_ref, out_ref):
    for x in range(N_X):
        rows = slice(64 * x, 64 * (x + 1))
        out_ref[x, 0:64, :] = (own_ref[rows, :].astype(F32) + other_ref[rows, :].astype(F32)).astype(BF16)
    lane = lax.broadcasted_iota(jnp.int32, (PACK, PAIR), 1)
    for piece in range(WIDTH // PACK):
        columns = slice(piece * PAIR, (piece + 1) * PAIR)
        partner = pltpu.roll(other_ref[256 : 256 + PACK, columns].astype(F32), BLOCK, 1)
        both = jnp.where(lane < BLOCK, pack_ref[:, columns].astype(F32), partner).astype(BF16)
        for x in range(N_X):
            out_ref[x, 64 : 64 + PACK, columns] = both


def own_half(own, pack, other):
    return pl.pallas_call(
        own_kernel,
        in_specs=[VMEM] * 3,
        out_specs=VMEM,
        out_shape=jax.ShapeDtypeStruct((N_X, 64 + PACK, D), BF16),
        compiler_params=SMALL,
        name="own_half",
    )(own, pack, other)


def spread_kernel(rank_ref, slot_ref, dest_ref, in_ref, ctx_ref, out_ref, ctx_out_ref, held_ref):
    total = in_ref[0, 0:64, :].astype(F32)
    for x in range(1, N_X):
        total = total + in_ref[x, 0:64, :].astype(F32)
    held_ref[...] = total
    upper = lax.broadcasted_iota(jnp.int32, (8, PAIR), 0) < 5
    for z in range(N_Z):
        rows = held_ref[5 * z : 5 * z + 8, :]
        late = rows[:, WIDE:]
        low, high = pltpu.roll(late, 5, 0), pltpu.roll(late, 2, 0)
        for piece in range(WIDE // PAIR):
            front = rows[:, piece * PAIR : (piece + 1) * PAIR]
            if piece < 6:
                source_piece = (high if piece % 2 else low)[:, piece // 2 * PAIR : (piece // 2 + 1) * PAIR]
                front = jnp.where(upper, front, source_piece)
            out_ref[z, :, piece * PAIR : (piece + 1) * PAIR] = front.astype(BF16)
    me = rank_ref[0]
    base = me // GROUP * GROUP
    source = base
    for k in range(1, GROUP):
        source = jnp.where(dest_ref[base + k] == me, base + k, source)
    slot = slot_ref[me]
    flip = (lax.rem(source, 2) != lax.rem(me, 2)) != (lax.rem(slot, 2) == 1)
    lane = lax.broadcasted_iota(jnp.int32, (PACK, PAIR), 1)
    mine = (lane >= BLOCK) == (lax.rem(slot, 2) == 1)
    x_source = lax.rem(source, 2 * N_X) // 2
    for part in range(WIDTH // PACK):
        rows = slice(part * PACK, (part + 1) * PACK)
        block_in = shifted(in_ref[x_source, 64 : 64 + PACK, part * PAIR : (part + 1) * PAIR], flip)
        ctx_out_ref[rows, :] = jnp.where(mine, block_in, ctx_ref[rows, :].astype(F32)).astype(BF16)


def spread(rank, slots, dest, received, ctx):
    tile = lambda i, rank, slots, dest: (0, slots[rank[0]] // 2)
    return pl.pallas_call(
        spread_kernel,
        grid_spec=pltpu.PrefetchScalarGridSpec(
            num_scalar_prefetch=3,
            grid=(1,),
            in_specs=[
                pl.BlockSpec((N_X, 64 + PACK, D), lambda i, rank, slots, dest: (0, 0, 0)),
                pl.BlockSpec((WIDTH, PAIR), tile),
            ],
            out_specs=[
                pl.BlockSpec((N_Z, 8, WIDE), lambda i, rank, slots, dest: (0, 0, 0)),
                pl.BlockSpec((WIDTH, PAIR), tile),
            ],
            scratch_shapes=[pltpu.VMEM((64, D), F32)],
        ),
        out_shape=[jax.ShapeDtypeStruct((N_Z, 8, WIDE), BF16), jax.ShapeDtypeStruct((WIDTH, ROWS), BF16)],
        input_output_aliases={4: 1},
        compiler_params=SMALL,
        name="spread",
    )(rank, slots, dest, received, ctx)


def last_kernel(in_ref, out_ref):
    total = in_ref[0].astype(F32)
    for z in range(1, N_Z):
        total = total + in_ref[z].astype(F32)
    out_ref[:, 0:WIDE] = total[0:5]
    upper = lax.broadcasted_iota(jnp.int32, (8, PAIR), 0) < 3
    for piece in range(3):
        low = pltpu.roll(total[:, 2 * piece * PAIR : (2 * piece + 1) * PAIR], 3, 0)
        high = pltpu.roll(total[:, (2 * piece + 1) * PAIR : (2 * piece + 2) * PAIR], 6, 0)
        out_ref[:, WIDE + piece * PAIR : WIDE + (piece + 1) * PAIR] = jnp.where(upper, low, high)[0:5]


def last_sum(received):
    return pl.pallas_call(
        last_kernel,
        in_specs=[VMEM],
        out_specs=VMEM,
        out_shape=jax.ShapeDtypeStruct((5, D), F32),
        compiler_params=SMALL,
        name="last_sum",
    )(received)


def shards(patches, qkv_weight, patch_counts, lend_dest, lend_slot, attn_grad):
    rank = lax.axis_index("dp").astype(jnp.int32).reshape(1)
    grad = attn_grad.T
    weight = qkv_weight.T
    groups = [[base + k for k in range(GROUP)] for base in range(0, N_DP, GROUP)]
    x_groups = [[z * 8 + x * 2 + core for x in range(N_X)] for z in range(N_Z) for core in range(2)]
    z_groups = [[z * 8 + place for z in range(N_Z)] for place in range(8)]
    gathered = lax.all_gather(pick(lend_slot, grad), "dp", axis=0, tiled=True, axis_index_groups=groups)
    ctx, terms, pack, *dqkv = block(rank, lend_slot, lend_dest, patch_counts, weight, patches, grad, gathered)
    summed = lax.psum_scatter(terms, "tensor", scatter_dimension=0, tiled=True)
    own, sent = sums(rank, patches, pack, dqkv)
    received = lax.ppermute(sent, "dp", [(p, p ^ 1) for p in range(N_DP)])
    parts = own_half(own, pack, received)
    parts = lax.all_to_all(parts, "dp", 0, 0, axis_index_groups=x_groups)
    parts, ctx = spread(rank, lend_slot, lend_dest, parts, ctx)
    parts = lax.all_to_all(parts, "dp", 0, 0, axis_index_groups=z_groups)
    return (ctx.T, summed.T, last_sum(parts))


def solution(mesh):
    return jax.shard_map(
        shards,
        mesh=mesh,
        in_specs=(P("dp", None), P(None, "tensor"), P(), P(), P(), P("dp", "tensor")),
        out_specs=(P("dp", "tensor"), P("dp", "tensor"), P(("tensor", "dp"), None)),
        check_vma=False,
    )
```
